32 devices in a mesh: parts: 2 (over y), tensor: 4 (over z), replica: 4 (over x, core).
Axes of the slice: x: 2, y: 2, z: 4, core: 2. Of those that a mesh axis runs over, the one named last changes fastest.
Arguments:
- attention_head_outputs: bfloat16 [2048, 4096], P(('parts', 'replica'), 'tensor'), parts along dimension 0, may hold values from -6 to 6
- group_owner_replica: int32 [128, 1], P(('parts', 'replica')), parts along dimension 0, may hold values from 0 to 3; in each aligned block of 16 rows (0 to 15, 16 to 31, ...) at most 4 rows name the same one
- group_adapter_slot: int32 [128], P(('parts', 'replica')), parts along dimension 0, may hold values from 0 to 7
- group_live_count: int32 [8, 16], P(('parts', 'replica')), parts along dimension 0, may hold values from 1 to 16, 224 in all within a row
- output_projection_weight: bfloat16 [4096, 8192], P('tensor'), may hold values from -0.125 to 0.125
- adapter_down_weight: bfloat16 [32, 64, 4096], P('replica', None, 'tensor'), may hold values from -0.09375 to 0.09375
- adapter_up_weight: bfloat16 [32, 64, 8192], P('replica', None, 'tensor'), may hold values from -0.75 to 0.75
Outputs:
- projected: bfloat16 [2048, 8192], P(('parts', 'replica')), parts along dimension 0
The draws below stay inside these ranges and needn't reach their ends.
There are 2 independent parts, one for each index of `parts`. The reference program is written for one: setup_inputs(seed, part) draws one part's arguments, and reference() takes and returns one part's arrays. A program takes and returns all parts, laid end to end along the dimension named above; an argument that names none is the same for every part. Nothing has to cross between parts.
Inputs may be any that keep to these rules, and one draw needn't show every extreme that they name: `group_owner_replica`: among the 16 groups of one index of replica, no owner is named more than 4 times.
All inputs are finite; a program needn't handle non-finite values.
Results may differ from the reference program's by a relative error of at most 0.013.
Values may be sent and summed in bfloat16 or wider, within the bound.
No kernel may reach another device: no remote copies, remote signals or barrier semaphores. Data moves between devices by JAX's collectives and lax.ppermute only.
A program may use at most 128 MiB of HBM per device.

```python
import math
import jax
import jax.numpy as jnp
import numpy as np
from jax import lax

INPUT_FEATURES = 4096
MODEL_WIDTH = 8192
ADAPTER_RANK = 64
GROUP_ROWS = 16
GROUP_DEV = 16
ADP_DEV = 8
CAP = 4
REQUESTS = 1024
GROUPS = 64
ADAPTER_TOTAL = 32
N_TENSOR = 4
N_REPLICA = 4


def place_ends(entries, key, smallest, largest):
    longest = entries.shape.index(max(entries.shape))
    spots = []
    for shift in (0, 1):
        where = [jax.random.randint(jax.random.fold_in(key, axis), (), 0, length) for axis, length in enumerate(entries.shape)]
        where[longest] = (where[longest] + shift) % entries.shape[longest]
        spots.append(tuple(where))
    return entries.at[spots[0]].set(smallest).at[spots[1]].set(largest)


def spiked(array, key, source, target, shards_of, factor):
    owner, partner = [(jnp.arange(array.shape[dim]) // (array.shape[dim] // shards_of)).reshape([-1 if axis == dim else 1 for axis in range(array.ndim)]) for dim in (source, target)]
    chosen = jax.random.permutation(key, shards_of)[partner]
    strong = (owner == chosen) | (owner == (partner + shards_of // 2) % shards_of)
    return jnp.where(strong, factor * array, array)


def steps_of(rng, shape, pieces, smallest, largest):
    def one(dim, shards_of):
        steps = jax.random.uniform(jax.random.fold_in(jax.random.fold_in(rng, 6), dim), (shards_of,), jnp.float32, smallest / len(pieces), largest / len(pieces))
        return jnp.repeat(jnp.exp(steps), shape[dim] // shards_of).reshape((-1,) + (1,) * (len(shape) - dim - 1))

    loudness = one(*pieces[0])
    for cut in pieces[1:]:
        loudness = loudness * one(*cut)
    return loudness


def length_profile(amount, total, bound, skew):
    weights = [(1 << 20) // math.isqrt(grade ** skew) + 1 for grade in range(2, amount + 1)]
    spare, given = total - bound - (amount - 1), [1] * (amount - 1)
    while spare > 0:
        candidates = [i for i in range(amount - 1) if given[i] < bound]
        pool, left = sum([weights[i] for i in candidates]), spare
        for i in candidates:
            more = min(bound - given[i], max(1, left * weights[i] // pool), spare)
            given[i] = given[i] + more
            spare = spare - more
    return np.array([bound] + given)


def uneven(own_key, amount, total, limit, slope):
    if amount == 2:
        one = jax.random.randint(own_key, (), max(1, total - limit), min(limit, total - 1) + 1)
        return jnp.stack([one, total - one])
    lengths = jnp.asarray(length_profile(amount, total, limit, slope), jnp.int32)
    twos = (amount - 1) // 2
    source_of, taker = lengths[1:1 + 2 * twos:2], lengths[2:2 + 2 * twos:2]
    room = jnp.minimum(source_of - 1, limit - taker)
    shifted = jax.random.randint(jax.random.fold_in(own_key, 1), (twos,), 0, 1 << 20) % (room + 1)
    lengths = lengths.at[1:1 + 2 * twos:2].set(source_of - shifted).at[2:2 + 2 * twos:2].set(taker + shifted)
    return lengths[jax.random.permutation(jax.random.fold_in(own_key, 2), amount)]


def assign_block(key, own, number, rows, number_of, top, most, skew):
    order = jax.random.permutation(key, number_of)
    crowded, ordinary = shares(number_of, rows * top, most, skew, True), shares(number_of, rows * top, most, skew, False)
    places = jnp.arange(number_of)

    def named(tallies, rotation):
        used = int((tallies > 0).sum())
        fixed = max(1, used // 4)
        shifted = fixed + (places - fixed + rotation * (used - fixed)) % max(1, number_of - fixed)
        return jnp.zeros((number_of,), jnp.int32).at[order[jnp.where(places < fixed, places, shifted)]].set(jnp.asarray(tallies, jnp.int32))

    tallies = jnp.where(number % 4 == 0, named(crowded, number // 4), named(ordinary, number - number // 4 - 1))
    mixed = jax.random.permutation(jax.random.fold_in(own, 3), number_of)
    donor, sink = mixed[0:number_of // 2 * 2:2], mixed[1:number_of // 2 * 2:2]
    room = jnp.minimum(tallies[donor] - 1, most - tallies[sink]) // 2
    room = jnp.where((donor == order[0]) | (sink == order[0]) | (tallies[sink] == 0), 0, jnp.maximum(room, 0))
    shifted = jax.random.randint(jax.random.fold_in(own, 4), (number_of // 2,), 0, 1 << 20) % (room + 1)
    tallies = tallies.at[donor].add(-shifted).at[sink].add(shifted)
    labels = jnp.searchsorted(jnp.cumsum(tallies), jnp.arange(rows * top), side="right").astype(jnp.int32)
    table = labels.reshape(top, rows).T
    table = table[jax.random.permutation(jax.random.fold_in(own, 1), rows)]
    rotation = jax.random.randint(jax.random.fold_in(own, 2), (rows, 1), 0, top)
    return jnp.take_along_axis(table, (jnp.arange(top)[None, :] + rotation) % top, axis=1)


def shares(number_of, total, limit, skew, full):
    loads = [(1 << 20) // math.isqrt(grade ** skew) + 1 for grade in range(1, number_of + 1)]
    largest = limit if full else min(limit, max(-(-total // number_of), total * loads[0] // sum(loads)))
    least = 1 if total - largest >= number_of - 1 else 0
    counts, surplus = [largest] + [least] * (number_of - 1), total - largest - least * (number_of - 1)
    while surplus > 0:
        free = [i for i in range(1, number_of) if counts[i] < largest] or [i for i in range(1, number_of) if counts[i] < limit]
        whole, budget = sum([loads[i] for i in free]), surplus
        for i in free:
            extra = min(limit - counts[i], max(1, budget * loads[i] // whole), surplus)
            counts[i] = counts[i] + extra
            surplus = surplus - extra
    return np.array(counts)


def bell_draw(rng, dims, deviation, most, shards=(), kind=jnp.bfloat16):
    entries = deviation * jax.random.normal(rng, dims, jnp.float32)
    if shards:
        entries = entries * steps_of(rng, dims, shards, -0.22, 0.18)
    return jnp.clip(entries, -most, most).astype(kind)


def noise_with(own_key, extent, scale, bound, shards, heavy, held_as=jnp.bfloat16):
    values = scale * jax.random.normal(own_key, extent, jnp.float32)
    if shards:
        values = values * steps_of(own_key, extent, shards, -0.22, 0.18)
    return jnp.clip(spiked(values, jax.random.fold_in(own_key, 3), *heavy), -bound, bound).astype(held_as)


def setup_inputs(seed: int = 0, part: int = 0) -> dict:
    streams_of = jax.random.split(jax.random.key(seed), 8)
    own_keys = jax.random.split(jax.random.fold_in(streams_of[7], part), 8)
    attention_head_outputs = bell_draw(own_keys[0], (REQUESTS, INPUT_FEATURES), 1.0, 6.0, ((0, 4), (1, 4)))
    group_owner_replica_keys = jax.random.split(jax.random.fold_in(own_keys[1], 1), GROUPS // GROUP_DEV)
    group_owner_replica_turns = jax.random.permutation(jax.random.fold_in(own_keys[1], 3), GROUPS // GROUP_DEV)
    group_owner_replica = jax.vmap(lambda own, number: assign_block(jax.random.fold_in(own_keys[1], 2), own, number, GROUP_DEV, N_REPLICA, 1, CAP, 2))(group_owner_replica_keys, group_owner_replica_turns).reshape((GROUPS, 1))
    group_adapter_slot = place_ends(jax.random.randint(own_keys[2], (GROUPS,), 0, ADP_DEV), jax.random.fold_in(own_keys[2], 1), 0, ADP_DEV - 1).astype(jnp.int32)
    group_live_count = jax.vmap(lambda own: uneven(own, GROUP_DEV, 14 * GROUP_DEV, 16, 1))(jax.random.split(own_keys[3], N_REPLICA)).reshape((N_REPLICA, GROUP_DEV)).astype(jnp.int32)
    output_projection_weight = noise_with(streams_of[4], (INPUT_FEATURES, MODEL_WIDTH), INPUT_FEATURES ** -0.5, 0.125, ((0, 4),), (0, 1, 4, 2.0))
    adapter_down_weight = bell_draw(streams_of[5], (ADAPTER_TOTAL, ADAPTER_RANK, INPUT_FEATURES), INPUT_FEATURES ** -0.5, 0.09375, ((0, 4), (2, 4)))
    adapter_up_weight = bell_draw(streams_of[6], (ADAPTER_TOTAL, ADAPTER_RANK, MODEL_WIDTH), ADAPTER_RANK ** -0.5, 0.75, ((0, 4), (2, 4)))
    return {"attention_head_outputs": attention_head_outputs, "group_owner_replica": group_owner_replica, "group_adapter_slot": group_adapter_slot, "group_live_count": group_live_count, "output_projection_weight": output_projection_weight, "adapter_down_weight": adapter_down_weight, "adapter_up_weight": adapter_up_weight}


def reference(attention_head_outputs, group_owner_replica, group_adapter_slot, group_live_count, output_projection_weight, adapter_down_weight, adapter_up_weight):
    block = INPUT_FEATURES // N_TENSOR

    def add_block(step, total):
        start = (step * block).astype(jnp.int32)
        inputs = lax.dynamic_slice_in_dim(attention_head_outputs, start, block, 1)
        weights = lax.dynamic_slice_in_dim(output_projection_weight, start, block, 0)
        term = jnp.dot(inputs, weights, preferred_element_type=jnp.float32).astype(jnp.bfloat16)
        term = lax.optimization_barrier(term)
        return total + term.astype(jnp.float32)

    base = lax.fori_loop(jnp.int32(0), jnp.int32(N_TENSOR), add_block, jnp.zeros((REQUESTS, MODEL_WIDTH), jnp.float32))
    adapter_index = (group_owner_replica[:, 0] * ADP_DEV + group_adapter_slot).astype(jnp.int32)
    grouped = attention_head_outputs.reshape(GROUPS, GROUP_ROWS, INPUT_FEATURES).astype(jnp.float32)
    shrink_row_block = jnp.take(adapter_down_weight, adapter_index, axis=0).astype(jnp.float32)
    low = jnp.einsum("gid,grd->gir", grouped, shrink_row_block).astype(jnp.bfloat16)
    expand_row_block = jnp.take(adapter_up_weight, adapter_index, axis=0).astype(jnp.float32)
    delta = jnp.einsum("gir,grn->gin", low.astype(jnp.float32), expand_row_block).reshape(REQUESTS, MODEL_WIDTH)
    sizes = group_live_count.reshape(GROUPS)
    live = (jnp.arange(GROUP_ROWS, dtype=jnp.int32)[None, :] < sizes[:, None]).reshape(REQUESTS, 1)
    return jnp.where(live, base + delta, jnp.float32(0.0)).astype(jnp.bfloat16)
```

```python
import functools

import jax
import jax.numpy as jnp
from jax import lax
from jax.experimental import pallas as pl
from jax.experimental.pallas import tpu as pltpu
from jax.sharding import PartitionSpec as P

GROUP_ROWS = 16
CAP = 4
LIVE_ROWS = 224
TAG = 128
CHUNK = 512
SKEW = 2
BF16 = jnp.bfloat16
F32 = jnp.float32
VMEM_BYTES = 40 * 1024 * 1024


def dot(a, b):
    return jnp.dot(a, b, preferred_element_type=F32)


def dot_rows(a, b):
    return lax.dot_general(a, b, (((0,), (0,)), ((), ())), preferred_element_type=F32)


def dot_cols(a, b):
    return lax.dot_general(a, b, (((1,), (1,)), ((), ())), preferred_element_type=F32)


def iota(shape, dim):
    return lax.broadcasted_iota(jnp.int32, shape, dim)


def params():
    return pltpu.CompilerParams(vmem_limit_bytes=VMEM_BYTES)


def prepare_kernel(replicas, owner, slot, live, me, x, compact_x, sent, pick, place):
    rows, feat = x.shape
    groups = rows // GROUP_ROWS
    out_rows = sent.shape[0]
    lane = iota((1, rows), 1)
    lane_group, lane_slot = lane // GROUP_ROWS, lane % GROUP_ROWS
    row_group = iota((rows, TAG), 0) // GROUP_ROWS
    packed = jnp.full((1, rows), -1, jnp.int32)
    target = jnp.zeros((1, rows), jnp.int32)
    tags = jnp.zeros((rows, TAG), F32)
    owners = [owner[g] for g in range(groups)]
    offset = jnp.int32(0)
    used = [jnp.int32(0)] * replicas
    for g in range(groups):
        count = live[g]
        mine = lane_group == g
        packed = jnp.where(mine & (lane_slot < count), offset + lane_slot, packed)
        offset = offset + count
        position = jnp.int32(0)
        for o in range(replicas):
            hit = owners[g] == o
            position = jnp.where(hit, used[o], position)
            used[o] = used[o] + hit.astype(jnp.int32)
        hop = lax.rem(owners[g] - me[0] + replicas, replicas)
        start = (hop * CAP + position) * GROUP_ROWS
        target = jnp.where(mine, start + lane_slot, target)
        tags = jnp.where(row_group == g, slot[g].astype(F32), tags)
    compact = (iota((LIVE_ROWS, rows), 0) == packed).astype(BF16)
    spread = (iota((out_rows, rows), 0) == target).astype(BF16)
    pick[...] = compact
    place[...] = dot_cols(compact, spread).astype(BF16)
    compact_x[...] = dot(compact, x[...]).astype(BF16)
    sent[:, :feat] = dot(spread, x[...]).astype(BF16)
    sent[:, feat:] = dot(spread, tags.astype(BF16)).astype(BF16)


def prepare(owner, slot, live, me, x, replicas):
    rows, feat = x.shape
    out_rows = replicas * CAP * GROUP_ROWS
    smem = pl.BlockSpec(memory_space=pltpu.SMEM)
    vmem = pl.BlockSpec(memory_space=pltpu.VMEM)
    return pl.pallas_call(
        functools.partial(prepare_kernel, replicas),
        out_shape=(
            jax.ShapeDtypeStruct((LIVE_ROWS, feat), BF16),
            jax.ShapeDtypeStruct((out_rows, feat + TAG), BF16),
            jax.ShapeDtypeStruct((LIVE_ROWS, rows), BF16),
            jax.ShapeDtypeStruct((LIVE_ROWS, out_rows), BF16),
        ),
        in_specs=[smem, smem, smem, smem, vmem],
        out_specs=(vmem,) * 4,
        compiler_params=params(),
        name="prepare",
    )(owner, slot, live, me, x)


def base_kernel(first, x, w, out):
    out[...] = dot(x[...], w[...]).astype(BF16)[None]


def base_chunks(first, x, weight, number):
    feat, width = weight.shape
    return pl.pallas_call(
        base_kernel,
        out_shape=jax.ShapeDtypeStruct((number, LIVE_ROWS, CHUNK), BF16),
        grid_spec=pltpu.PrefetchScalarGridSpec(
            num_scalar_prefetch=1,
            grid=(number,),
            in_specs=[
                pl.BlockSpec((LIVE_ROWS, feat), lambda i, first: (0, 0)),
                pl.BlockSpec((feat, CHUNK), lambda i, first: (0, first[0] + i)),
            ],
            out_specs=pl.BlockSpec((1, LIVE_ROWS, CHUNK), lambda i, first: (i, 0, 0)),
        ),
        compiler_params=params(),
        cost_estimate=pl.CostEstimate(
            flops=2 * LIVE_ROWS * feat * CHUNK * number,
            bytes_accessed=2 * (feat + LIVE_ROWS) * CHUNK * number,
            transcendentals=0,
        ),
        name="base",
    )(first, x, weight)


def fold(rank, adapters, half):
    shape = (adapters * rank, 2 * rank)
    return (iota(shape, 0) % rank + half * rank == iota(shape, 1)).astype(BF16)


def slot_mask(tag, rank, adapters):
    shape = (tag.shape[0], adapters * rank)
    return (iota(shape, 1) // rank).astype(F32) == tag.astype(F32)


def low_kernel(rank, blocks, down, *refs):
    parts, low = refs[:blocks], refs[blocks]
    adapters = down.shape[0] // rank
    feat = down.shape[1]
    rows = parts[0].shape[0]
    half = blocks // 2
    maps = down[...]
    folds = [fold(rank, adapters, h) for h in range(2)]
    for k in range(half):
        total = None
        for h in range(2):
            part = parts[h * half + k]
            wide = dot_cols(part[:, :feat], maps)
            kept = jnp.where(slot_mask(part[:, feat : feat + 1], rank, adapters), wide, 0.0)
            got = dot(kept.astype(BF16), folds[h])
            total = got if total is None else total + got
        low[k * rows : (k + 1) * rows, :] = total.astype(BF16)


def low_values(parts, down, rank):
    rows, width = parts[0].shape
    blocks = len(parts)
    vmem = pl.BlockSpec(memory_space=pltpu.VMEM)
    return pl.pallas_call(
        functools.partial(low_kernel, rank, blocks),
        out_shape=jax.ShapeDtypeStruct((blocks // 2 * rows, 2 * rank), BF16),
        in_specs=[vmem] * (blocks + 1),
        out_specs=vmem,
        compiler_params=params(),
        name="low",
    )(down, *parts)


def delta_kernel(rank, blocks, sums, up, *refs):
    tags, lows, outs = refs[:blocks], refs[blocks : blocks + sums], refs[blocks + sums :]
    adapters = up.shape[0] // rank
    rows = tags[0].shape[0]
    half = blocks // 2
    total = lows[0][...].astype(F32)
    for other in lows[1:]:
        total = total + other[...].astype(F32)
    low = total.astype(BF16)
    maps = up[...]
    for h in range(2):
        spread = fold(rank, adapters, h)
        for k in range(half):
            wide = dot_cols(low[k * rows : (k + 1) * rows, :], spread)
            mask = slot_mask(tags[h * half + k][:, :1], rank, adapters)
            kept = jnp.where(mask, wide, 0.0).astype(BF16)
            outs[h * half + k][...] = dot(kept, maps).astype(BF16)


def delta_values(parts, lows, up, rank):
    rows, width = parts[0].shape
    blocks = len(parts)
    columns = up.shape[1]
    vmem = pl.BlockSpec(memory_space=pltpu.VMEM)
    tag = pl.BlockSpec((rows, TAG), lambda i: (0, width // TAG - 1))
    whole = lambda a: pl.BlockSpec(a.shape, lambda i: (0, 0))
    return pl.pallas_call(
        functools.partial(delta_kernel, rank, blocks, len(lows)),
        out_shape=[jax.ShapeDtypeStruct((rows, columns), BF16)] * blocks,
        grid=(1,),
        in_specs=[whole(up)] + [tag] * blocks + [whole(a) for a in lows],
        out_specs=[pl.BlockSpec((rows, columns), lambda i: (0, 0))] * blocks,
        compiler_params=params(),
        name="delta",
    )(up, *parts, *lows)


def add_delta_kernel(blocks, first, base, place, *refs):
    parts, out = refs[:blocks], refs[blocks]
    rows = parts[0].shape[0]
    total = base[0].astype(F32)
    for k in range(blocks):
        total = total + dot(place[:, k * rows : (k + 1) * rows], parts[k][...])
    out[0] = total.astype(BF16)


def add_delta(first, base, place, parts):
    rows, columns = parts[0].shape
    chunk = base.shape[2]
    return pl.pallas_call(
        functools.partial(add_delta_kernel, len(parts)),
        out_shape=jax.ShapeDtypeStruct((columns // chunk, LIVE_ROWS, chunk), BF16),
        grid_spec=pltpu.PrefetchScalarGridSpec(
            num_scalar_prefetch=1,
            grid=(columns // chunk,),
            in_specs=[
                pl.BlockSpec((1, LIVE_ROWS, chunk), lambda i, first: (first[0] + i, 0, 0)),
                pl.BlockSpec(place.shape, lambda i, first: (0, 0)),
            ]
            + [pl.BlockSpec((rows, chunk), lambda i, first: (0, i))] * len(parts),
            out_specs=pl.BlockSpec((1, LIVE_ROWS, chunk), lambda i, first: (i, 0, 0)),
        ),
        compiler_params=params(),
        name="add_delta",
    )(first, base, place, *parts)


def finish_kernel(at, base, left, right, pick, held, out):
    @pl.when(at[1] > 0)
    def _():
        total = base[...].astype(F32) + left[...].astype(F32) + right[...].astype(F32)
        out[...] = dot_rows(pick[...], total.astype(BF16)).astype(BF16)

    @pl.when(at[1] == 0)
    def _():
        out[...] = held[...]


def finish(at, base, left, right, pick, held):
    rows = pick.shape[1]
    whole = lambda a: pl.BlockSpec(a.shape, lambda i, at: (0,) * a.ndim)
    here = pl.BlockSpec((rows, CHUNK), lambda i, at: (0, at[0]))
    return pl.pallas_call(
        finish_kernel,
        out_shape=jax.ShapeDtypeStruct(held.shape, BF16),
        grid_spec=pltpu.PrefetchScalarGridSpec(
            num_scalar_prefetch=1,
            grid=(1,),
            in_specs=[whole(base), whole(left), whole(right), whole(pick), here],
            out_specs=here,
        ),
        input_output_aliases={5: 0},
        compiler_params=params(),
        name="finish",
    )(at, base, left, right, pick, held)


def adapter_parts(sent, down, up):
    replicas, shards = lax.axis_size("replica"), lax.axis_size("tensor")
    rank = down.shape[1]
    rows = CAP * GROUP_ROWS
    parts = [sent[:rows]]
    for k in range(1, replicas):
        hops = [(i, (i + k) % replicas) for i in range(replicas)]
        parts.append(lax.ppermute(sent[k * rows : (k + 1) * rows], "replica", hops))
    low = low_values(parts, down.reshape(-1, down.shape[2]), rank)
    if shards <= 4:
        lows = [low]
        for k in range(1, shards):
            hops = [(i, (i + k) % shards) for i in range(shards)]
            lows.append(lax.ppermute(low, "tensor", hops))
    else:
        lows = [lax.psum(low, "tensor")]
    made = delta_values(parts, lows, up.reshape(-1, up.shape[2]), rank)
    back = [made[0]]
    for k in range(1, replicas):
        hops = [(i, (i - k) % replicas) for i in range(replicas)]
        back.append(lax.ppermute(made[k], "replica", hops))
    return back


def on_device(x, owner, slot, live, weight, down, up):
    rows = x.shape[0]
    width = weight.shape[1]
    replicas, shards = lax.axis_size("replica"), lax.axis_size("tensor")
    me = lax.axis_index("replica").astype(jnp.int32).reshape(1)
    z = lax.axis_index("tensor").astype(jnp.int32)
    compact_x, sent, pick, place = prepare(owner[:, 0], slot, live[0], me, x, replicas)
    share = width // shards
    if shards != 4:
        base = dot(compact_x, weight)
        back = jnp.concatenate(adapter_parts(sent, down, up), axis=0)
        mine = lax.dynamic_slice_in_dim(base, z * share, share, 1) + dot(place, back)
        base = lax.dynamic_update_slice_in_dim(base, mine, z * share, 1).astype(BF16)
        total = lax.psum_scatter(base, "tensor", scatter_dimension=1, tiled=True)
        total = lax.all_gather(total, "tensor", axis=1, tiled=True)
        return dot_rows(pick, total).astype(BF16)

    chunks, per = width // CHUNK, share // CHUNK
    last = shards - 1
    even_right = z % 2 == 0
    right_lag, left_lag = -SKEW * z, -SKEW * (last - z)

    def chunk_of(position, right):
        return jnp.clip(jnp.where(right, chunks - 1 - position, position), 0, chunks - 1)

    def even_chunk(step):
        return chunk_of(step + jnp.where(even_right, right_lag, left_lag), even_right)

    def odd_chunk(step):
        return chunk_of(step + jnp.where(even_right, left_lag, right_lag), ~even_right)

    even = [pair for i in range(0, last, 2) for pair in ((i, i + 1), (i + 1, i))]
    odd = [pair for i in range(1, last, 2) for pair in ((i, i + 1), (i + 1, i))]
    first = base_chunks(even_chunk(0).reshape(1), compact_x, weight, 1)[0]
    base = base_chunks(jnp.zeros((1,), jnp.int32), compact_x, weight, chunks)
    back = adapter_parts(sent, down, up)
    own = add_delta((z * per).reshape(1), base, place, back)

    def term(chunk, with_delta):
        plain = lax.dynamic_index_in_dim(base, chunk, 0, keepdims=False)
        if not with_delta:
            return plain
        near = lax.dynamic_index_in_dim(own, jnp.clip(chunk - z * per, 0, per - 1), 0, keepdims=False)
        return jnp.where(chunk // per == z, near, plain)

    steps = chunks + SKEW * (shards - 2)
    ready = per + SKEW * (shards - 2)
    evens, odds = [], []
    result = jnp.zeros((rows, width), BF16)
    inner = (z > 0) & (z < last)

    def close(step, result):
        partner = chunks - 1 - step + SKEW
        got_odd = odds[partner] if 0 <= partner < len(odds) else jnp.zeros_like(evens[0])
        position = jnp.where(inner, step, step - SKEW * (shards - 2))
        chunk = chunk_of(position, ~even_right)
        valid = (position >= 0) & (position < chunks)
        at = jnp.stack([chunk, valid.astype(jnp.int32)])
        return finish(at, term(chunk, True), evens[step], got_odd, pick, result)

    for step in range(steps):
        with_delta = step >= ready
        if step == 0:
            message = first
        else:
            message = term(even_chunk(step), with_delta)
            if step >= SKEW:
                message = (message.astype(F32) + odds[step - SKEW].astype(F32)).astype(BF16)
        evens.append(lax.ppermute(message, "tensor", even))
        if step < SKEW:
            odds.append(jnp.zeros_like(first))
        elif step < chunks + SKEW:
            message = term(odd_chunk(step), with_delta)
            message = (message.astype(F32) + evens[step - SKEW].astype(F32)).astype(BF16)
            odds.append(lax.ppermute(message, "tensor", odd))
    done = set()
    for step in range(steps):
        for s in range(step + 1):
            partner = chunks - 1 - s + SKEW
            if s not in done and partner <= step:
                result = close(s, result)
                done.add(s)
    return result


def solution(mesh):
    placed = (
        P(("parts", "replica"), "tensor"),
        P(("parts", "replica"), None),
        P(("parts", "replica")),
        P(("parts", "replica"), None),
        P("tensor", None),
        P("replica", None, "tensor"),
        P("replica", None, "tensor"),
    )
    return jax.shard_map(
        on_device,
        mesh=mesh,
        in_specs=placed,
        out_specs=P(("parts", "replica"), None),
        check_vma=False,
    )
```

```python
import functools

import jax
import jax.numpy as jnp
from jax import lax
from jax.experimental import pallas as pl
from jax.experimental.pallas import tpu as pltpu
from jax.sharding import PartitionSpec as P

GROUP_ROWS = 16
CAP = 4
LIVE_ROWS = 224
TAG = 128
CHUNK = 1024
TILE = 512
BF16 = jnp.bfloat16
F32 = jnp.float32
MIB = 1024 * 1024


def dot(a, b):
    return jnp.dot(a, b, preferred_element_type=F32)


def dot_rows(a, b):
    return lax.dot_general(a, b, (((0,), (0,)), ((), ())), preferred_element_type=F32)


def dot_cols(a, b):
    return lax.dot_general(a, b, (((1,), (1,)), ((), ())), preferred_element_type=F32)


def iota(shape, dim):
    return lax.broadcasted_iota(jnp.int32, shape, dim)


def params(mib=16):
    return pltpu.CompilerParams(vmem_limit_bytes=mib * MIB)


def cost(flops, elements):
    return pl.CostEstimate(flops=flops, bytes_accessed=2 * elements, transcendentals=0)


ANY = pl.BlockSpec(memory_space=pl.ANY)
VMEM = pl.BlockSpec(memory_space=pltpu.VMEM)


def prepare_kernel(replicas, owner_in, slot_in, live_in, x, compact_x, sent, pick, place, owner, slot, live, sems):
    copies = [
        pltpu.make_async_copy(src, dst, sems.at[i])
        for i, (src, dst) in enumerate(((owner_in, owner), (slot_in, slot), (live_in, live)))
    ]
    for copy in copies:
        copy.start()
    for copy in copies:
        copy.wait()
    me = lax.axis_index("replica")
    rows, feat = x.shape
    groups = rows // GROUP_ROWS
    out_rows = sent.shape[0]
    lane = iota((1, rows), 1)
    lane_group, lane_slot = lane // GROUP_ROWS, lane % GROUP_ROWS
    row_group = iota((rows, TAG), 0) // GROUP_ROWS
    packed = jnp.full((1, rows), -1, jnp.int32)
    target = jnp.zeros((1, rows), jnp.int32)
    tags = jnp.zeros((rows, TAG), F32)
    owners = [owner[g] for g in range(groups)]
    offset = jnp.int32(0)
    used = [jnp.int32(0)] * replicas
    for g in range(groups):
        count = live[g]
        mine = lane_group == g
        packed = jnp.where(mine & (lane_slot < count), offset + lane_slot, packed)
        offset = offset + count
        position = jnp.int32(0)
        for o in range(replicas):
            hit = owners[g] == o
            position = jnp.where(hit, used[o], position)
            used[o] = used[o] + hit.astype(jnp.int32)
        hop = lax.rem(owners[g] - me + replicas, replicas)
        start = (hop * CAP + position) * GROUP_ROWS
        target = jnp.where(mine, start + lane_slot, target)
        tags = jnp.where(row_group == g, slot[g].astype(F32), tags)
    compact = (iota((LIVE_ROWS, rows), 0) == packed).astype(BF16)
    spread = (iota((out_rows, rows), 0) == target).astype(BF16)
    pick[...] = compact
    place[...] = dot_cols(compact, spread).astype(BF16)
    compact_x[...] = dot(compact, x[...]).astype(BF16)
    sent[:, :feat] = dot(spread, x[...]).astype(BF16)
    sent[:, feat:] = dot(spread, tags.astype(BF16)).astype(BF16)


def prepare(owner, slot, live, x, replicas):
    rows, feat = x.shape
    out_rows = replicas * CAP * GROUP_ROWS
    smalls = [pltpu.SMEM(a.shape, jnp.int32) for a in (owner, slot, live)]
    return pl.pallas_call(
        functools.partial(prepare_kernel, replicas),
        out_shape=(
            jax.ShapeDtypeStruct((LIVE_ROWS, feat), BF16),
            jax.ShapeDtypeStruct((out_rows, feat + TAG), BF16),
            jax.ShapeDtypeStruct((LIVE_ROWS, rows), BF16),
            jax.ShapeDtypeStruct((LIVE_ROWS, out_rows), BF16),
        ),
        in_specs=[ANY, ANY, ANY, VMEM],
        out_specs=(VMEM,) * 4,
        scratch_shapes=smalls + [pltpu.SemaphoreType.DMA((3,))],
        compiler_params=params(),
        name="prepare",
    )(owner, slot, live, x)


def first_kernel(at, x, w, out):
    out[...] = dot(x[...], w[...]).astype(BF16)


def first_chunk(at, x, weight):
    feat, _ = weight.shape
    tiles = CHUNK // TILE
    return pl.pallas_call(
        first_kernel,
        out_shape=jax.ShapeDtypeStruct((LIVE_ROWS, CHUNK), BF16),
        grid_spec=pltpu.PrefetchScalarGridSpec(
            num_scalar_prefetch=1,
            grid=(tiles,),
            in_specs=[
                pl.BlockSpec((LIVE_ROWS, feat), lambda i, at: (0, 0)),
                pl.BlockSpec((feat, TILE), lambda i, at: (0, at[0] * tiles + i)),
            ],
            out_specs=pl.BlockSpec((LIVE_ROWS, TILE), lambda i, at: (0, i)),
        ),
        compiler_params=params(48),
        cost_estimate=cost(2 * LIVE_ROWS * feat * CHUNK, (feat + LIVE_ROWS) * CHUNK),
        name="first",
    )(at, x, weight)


def base_kernel(x, w, token_in, out, token):
    wide = dot(x[...], w[...]).astype(BF16)
    for j in range(out.shape[0]):
        out[j] = wide[:, j * CHUNK : (j + 1) * CHUNK]


def base_chunks(x, weight, token, group=2):
    feat, width = weight.shape
    number = width // CHUNK
    return pl.pallas_call(
        base_kernel,
        out_shape=(
            jax.ShapeDtypeStruct((number, LIVE_ROWS, CHUNK), BF16),
            jax.ShapeDtypeStruct(token.shape, token.dtype),
        ),
        grid=(number // group,),
        in_specs=[
            pl.BlockSpec((LIVE_ROWS, feat), lambda i: (0, 0)),
            pl.BlockSpec((feat, group * CHUNK), lambda i: (0, i)),
            ANY,
        ],
        out_specs=(pl.BlockSpec((group, LIVE_ROWS, CHUNK), lambda i: (i, 0, 0)), ANY),
        input_output_aliases={2: 1},
        compiler_params=params(48),
        cost_estimate=cost(2 * LIVE_ROWS * feat * width, (feat + LIVE_ROWS) * width),
        name="base",
    )(x, weight, token)


def hop_kernel(at, base, *refs):
    out = refs[-2]
    total = base[0].astype(F32)
    if len(refs) == 4:
        total = total + refs[0][...].astype(F32)
    out[...] = total.astype(BF16)


def hop(chunk, base, got, token):
    here = pl.BlockSpec((LIVE_ROWS, TILE), lambda i, at: (0, i))
    inputs = [base] + ([got] if got is not None else []) + [token]
    return pl.pallas_call(
        hop_kernel,
        out_shape=(
            jax.ShapeDtypeStruct((LIVE_ROWS, CHUNK), BF16),
            jax.ShapeDtypeStruct(token.shape, token.dtype),
        ),
        grid_spec=pltpu.PrefetchScalarGridSpec(
            num_scalar_prefetch=1,
            grid=(CHUNK // TILE,),
            in_specs=[pl.BlockSpec((1, LIVE_ROWS, TILE), lambda i, at: (at[0], 0, i))]
            + [here] * (len(inputs) - 2)
            + [ANY],
            out_specs=(here, ANY),
        ),
        input_output_aliases={len(inputs): 1},
        compiler_params=params(),
        cost_estimate=cost(2 * LIVE_ROWS * CHUNK, 3 * LIVE_ROWS * CHUNK),
        name="hop",
    )(chunk.reshape(1), *inputs)


def fold(rank, adapters, half):
    shape = (adapters * rank, 2 * rank)
    return (iota(shape, 0) % rank + half * rank == iota(shape, 1)).astype(BF16)


def slot_mask(tag, rank, adapters):
    shape = (tag.shape[0], adapters * rank)
    return (iota(shape, 1) // rank).astype(F32) == tag.astype(F32)


def low_kernel(rank, blocks, down, *refs):
    parts, low = refs[:blocks], refs[blocks + 1]
    adapters = down.shape[0] // rank
    feat = down.shape[1]
    rows = parts[0].shape[0]
    half = blocks // 2
    maps = down[...]
    folds = [fold(rank, adapters, h) for h in range(2)]
    for k in range(half):
        total = None
        for h in range(2):
            part = parts[h * half + k]
            wide = dot_cols(part[:, :feat], maps)
            kept = jnp.where(slot_mask(part[:, feat : feat + 1], rank, adapters), wide, 0.0)
            got = dot(kept.astype(BF16), folds[h])
            total = got if total is None else total + got
        low[k * rows : (k + 1) * rows, :] = total.astype(BF16)


def low_values(parts, down, rank, token):
    rows, width = parts[0].shape
    blocks = len(parts)
    return pl.pallas_call(
        functools.partial(low_kernel, rank, blocks),
        out_shape=(
            jax.ShapeDtypeStruct((blocks // 2 * rows, 2 * rank), BF16),
            jax.ShapeDtypeStruct(token.shape, token.dtype),
        ),
        in_specs=[VMEM] * (blocks + 1) + [ANY],
        out_specs=(VMEM, ANY),
        input_output_aliases={blocks + 1: 1},
        compiler_params=params(),
        name="low",
    )(down, *parts, token)


def delta_kernel(rank, blocks, sums, up, *refs):
    tags, lows, outs = refs[:blocks], refs[blocks : blocks + sums], refs[blocks + sums + 1 :]
    adapters = up.shape[0] // rank
    rows = tags[0].shape[0]
    half = blocks // 2
    total = lows[0][...].astype(F32)
    for other in lows[1:]:
        total = total + other[...].astype(F32)
    low = total.astype(BF16)
    maps = up[...]
    for h in range(2):
        spread = fold(rank, adapters, h)
        for k in range(half):
            wide = dot_cols(low[k * rows : (k + 1) * rows, :], spread)
            mask = slot_mask(tags[h * half + k][:, :1], rank, adapters)
            kept = jnp.where(mask, wide, 0.0).astype(BF16)
            outs[h * half + k][...] = dot(kept, maps).astype(BF16)


def delta_values(parts, lows, up, rank, token):
    rows, width = parts[0].shape
    blocks = len(parts)
    columns = up.shape[1]
    tag = pl.BlockSpec((rows, TAG), lambda i: (0, width // TAG - 1))
    whole = lambda a: pl.BlockSpec(a.shape, lambda i: (0, 0))
    return pl.pallas_call(
        functools.partial(delta_kernel, rank, blocks, len(lows)),
        out_shape=[jax.ShapeDtypeStruct((rows, columns), BF16)] * blocks
        + [jax.ShapeDtypeStruct(token.shape, token.dtype)],
        grid=(1,),
        in_specs=[whole(up)] + [tag] * blocks + [whole(a) for a in lows] + [ANY],
        out_specs=[pl.BlockSpec((rows, columns), lambda i: (0, 0))] * blocks + [ANY],
        input_output_aliases={1 + blocks + len(lows): blocks},
        compiler_params=params(),
        name="delta",
    )(up, *parts, *lows, token)


def add_delta_kernel(blocks, at, base, place, *refs):
    parts, out = refs[:blocks], refs[blocks + 1]
    rows = parts[0].shape[0]
    total = base[0].astype(F32)
    for k in range(blocks):
        total = total + dot(place[:, k * rows : (k + 1) * rows], parts[k][...])
    out[0] = total.astype(BF16)


def add_delta(first, base, place, parts, token):
    rows, columns = parts[0].shape
    chunk = base.shape[2]
    here = pl.BlockSpec((1, LIVE_ROWS, chunk), lambda i, at: (at[0] + i, 0, 0))
    return pl.pallas_call(
        functools.partial(add_delta_kernel, len(parts)),
        out_shape=(
            jax.ShapeDtypeStruct(base.shape, base.dtype),
            jax.ShapeDtypeStruct(token.shape, token.dtype),
        ),
        grid_spec=pltpu.PrefetchScalarGridSpec(
            num_scalar_prefetch=1,
            grid=(columns // chunk,),
            in_specs=[here, pl.BlockSpec(place.shape, lambda i, at: (0, 0))]
            + [pl.BlockSpec((rows, chunk), lambda i, at: (0, i))] * len(parts)
            + [ANY],
            out_specs=(here, ANY),
        ),
        input_output_aliases={1: 0, 3 + len(parts): 1},
        compiler_params=params(),
        name="add_delta",
    )(first, base, place, *parts, token)


def finish_kernel(at, base, left, right, pick, held, token_in, out, token):
    @pl.when(at[1] > 0)
    def _():
        total = base[0].astype(F32) + left[...].astype(F32) + right[...].astype(F32)
        out[...] = dot_rows(pick[...], total.astype(BF16)).astype(BF16)

    @pl.when(at[1] == 0)
    def _():
        out[...] = held[...]


def finish(at, base, left, right, pick, held, token):
    rows = pick.shape[1]
    tiles = CHUNK // TILE
    got = pl.BlockSpec((LIVE_ROWS, TILE), lambda i, at: (0, i))
    here = pl.BlockSpec((rows, TILE), lambda i, at: (0, at[0] * tiles + i))
    return pl.pallas_call(
        finish_kernel,
        out_shape=(
            jax.ShapeDtypeStruct(held.shape, BF16),
            jax.ShapeDtypeStruct(token.shape, token.dtype),
        ),
        grid_spec=pltpu.PrefetchScalarGridSpec(
            num_scalar_prefetch=1,
            grid=(tiles,),
            in_specs=[
                pl.BlockSpec((1, LIVE_ROWS, TILE), lambda i, at: (at[0], 0, i)),
                got,
                got,
                pl.BlockSpec(pick.shape, lambda i, at: (0, 0)),
                here,
                ANY,
            ],
            out_specs=(here, ANY),
        ),
        input_output_aliases={5: 0, 6: 1},
        compiler_params=params(),
        cost_estimate=cost(2 * LIVE_ROWS * rows * CHUNK, 6 * LIVE_ROWS * CHUNK),
        name="finish",
    )(at, base, left, right, pick, held, token)


def send_groups(sent):
    replicas = lax.axis_size("replica")
    rows = CAP * GROUP_ROWS
    parts = [sent[:rows]]
    for k in range(1, replicas):
        hops = [(i, (i + k) % replicas) for i in range(replicas)]
        parts.append(lax.ppermute(sent[k * rows : (k + 1) * rows], "replica", hops))
    return parts


def send_lows(low):
    shards = lax.axis_size("tensor")
    if shards > 4:
        return [lax.psum(low, "tensor")]
    lows = [low]
    for k in range(1, shards):
        hops = [(i, (i + k) % shards) for i in range(shards)]
        lows.append(lax.ppermute(low, "tensor", hops))
    return lows


def send_back(made):
    replicas = lax.axis_size("replica")
    back = [made[0]]
    for k in range(1, replicas):
        hops = [(i, (i - k) % replicas) for i in range(replicas)]
        back.append(lax.ppermute(made[k], "replica", hops))
    return back


def on_device(x, owner, slot, live, weight, down, up):
    rows = x.shape[0]
    width = weight.shape[1]
    rank = down.shape[1]
    replicas, shards = lax.axis_size("replica"), lax.axis_size("tensor")
    z = lax.axis_index("tensor").astype(jnp.int32)
    compact_x, sent, pick, place = prepare(owner[:, 0], slot, live[0], x, replicas)
    share = width // shards
    down, up = down.reshape(-1, down.shape[2]), up.reshape(-1, up.shape[2])
    token = jnp.zeros((8, 128), jnp.int32)
    if shards != 4:
        base = dot(compact_x, weight)
        parts = send_groups(sent)
        low, token = low_values(parts, down, rank, token)
        *made, token = delta_values(parts, send_lows(low), up, rank, token)
        back = jnp.concatenate(send_back(made), axis=0)
        mine = lax.dynamic_slice_in_dim(base, z * share, share, 1) + dot(place, back)
        base = lax.dynamic_update_slice_in_dim(base, mine, z * share, 1).astype(BF16)
        total = lax.psum_scatter(base, "tensor", scatter_dimension=1, tiled=True)
        total = lax.all_gather(total, "tensor", axis=1, tiled=True)
        return dot_rows(pick, total).astype(BF16)

    chunks, per = width // CHUNK, share // CHUNK
    inner = (z == 1) | (z == 2)
    even_right, odd_right = z % 2 == 0, z % 2 == 1
    even = [(0, 1), (1, 0), (2, 3), (3, 2)]
    odd = [(1, 2), (2, 1)]

    def chunk_of(position, right):
        return jnp.clip(jnp.where(right, chunks - 1 - position, position), 0, chunks - 1)

    def even_chunk(step):
        return chunk_of(step - jnp.where(inner, 3, 0), even_right)

    def odd_chunk(step):
        return chunk_of(jnp.int32(step - 1), odd_right)

    evens, odds = {}, {}
    result = jnp.zeros((rows, width), BF16)
    message = first_chunk(even_chunk(0).reshape(1), compact_x, weight)
    evens[0] = lax.ppermute(message, "tensor", even)
    parts = send_groups(sent)
    base, token = base_chunks(compact_x, weight, token)
    unfinished = list(range(chunks + 3))
    seen_even, seen_odd = set(), set()

    def close(result, token, base):
        for a in list(unfinished):
            b = chunks - a
            if a not in seen_even or (1 <= b <= chunks and b not in seen_odd):
                continue
            unfinished.remove(a)
            position = jnp.where(inner, a, a - 3)
            valid = (position >= 0) & (position < chunks)
            at = jnp.stack([chunk_of(position, ~even_right), valid.astype(jnp.int32)])
            other = odds[b] if 1 <= b <= chunks else odds[1]
            result, token = finish(at, base, evens[a], other, pick, result, token)
        return result, token

    for step in range(1, chunks + 3):
        message, token = hop(even_chunk(step), base, odds.get(step - 2), token)
        evens[step] = lax.ppermute(message, "tensor", even)
        seen_odd.add(step - 2)
        if step == 1:
            low, token = low_values(parts, down, rank, token)
            lows = send_lows(low)
        if step == 2:
            *made, token = delta_values(parts, lows, up, rank, token)
            back = send_back(made)
        if step == 3 + per - 1:
            base, token = add_delta((z * per).reshape(1), base, place, back, token)
        result, token = close(result, token, base)
        if step <= chunks:
            message, token = hop(odd_chunk(step), base, evens[step - 1], token)
            odds[step] = lax.ppermute(message, "tensor", odd)
        seen_even.add(step - 1)
        result, token = close(result, token, base)
    seen_even.add(chunks + 2)
    result, token = close(result, token, base)
    return result


def solution(mesh):
    placed = (
        P(("parts", "replica"), "tensor"),
        P(("parts", "replica"), None),
        P(("parts", "replica")),
        P(("parts", "replica"), None),
        P("tensor", None),
        P("replica", None, "tensor"),
        P("replica", None, "tensor"),
    )
    return jax.shard_map(
        on_device,
        mesh=mesh,
        in_specs=placed,
        out_specs=P(("parts", "replica"), None),
        check_vma=False,
    )
```

```python
import functools

import jax
import jax.numpy as jnp
from jax import lax
from jax.experimental import pallas as pl
from jax.experimental.pallas import tpu as pltpu
from jax.sharding import PartitionSpec as P

GROUP_ROWS = 16
CAP = 4
LIVE_ROWS = 224
TAG = 128
CHUNK = 1024
TILE = 512
BF16 = jnp.bfloat16
F32 = jnp.float32
MIB = 1024 * 1024


def dot(a, b):
    return jnp.dot(a, b, preferred_element_type=F32)


def dot_cols(a, b):
    return lax.dot_general(a, b, (((1,), (1,)), ((), ())), preferred_element_type=F32)


def iota(shape, dim):
    return lax.broadcasted_iota(jnp.int32, shape, dim)


def params(mib=50):
    return pltpu.CompilerParams(vmem_limit_bytes=mib * MIB)


def cost(flops, elements):
    return pl.CostEstimate(flops=flops, bytes_accessed=2 * elements, transcendentals=0)


ANY = pl.BlockSpec(memory_space=pl.ANY)
VMEM = pl.BlockSpec(memory_space=pltpu.VMEM)


def prepare_kernel(replicas, owner_in, slot_in, live_in, x, compact_x, sent, pick, place, owner, slot, live, sems):
    copies = [
        pltpu.make_async_copy(src, dst, sems.at[i])
        for i, (src, dst) in enumerate(((owner_in, owner), (slot_in, slot), (live_in, live)))
    ]
    for copy in copies:
        copy.start()
    for copy in copies:
        copy.wait()
    me = lax.axis_index("replica")
    rows, feat = x.shape
    groups = rows // GROUP_ROWS
    out_rows = sent.shape[0]
    lane = iota((1, rows), 1)
    lane_group, lane_slot = lane // GROUP_ROWS, lane % GROUP_ROWS
    row_group = iota((rows, TAG), 0) // GROUP_ROWS
    packed = jnp.full((1, rows), -1, jnp.int32)
    target = jnp.zeros((1, rows), jnp.int32)
    tags = jnp.zeros((rows, TAG), F32)
    owners = [owner[g] for g in range(groups)]
    offset = jnp.int32(0)
    used = [jnp.int32(0)] * replicas
    for g in range(groups):
        count = live[g]
        mine = lane_group == g
        packed = jnp.where(mine & (lane_slot < count), offset + lane_slot, packed)
        offset = offset + count
        position = jnp.int32(0)
        for o in range(replicas):
            hit = owners[g] == o
            position = jnp.where(hit, used[o], position)
            used[o] = used[o] + hit.astype(jnp.int32)
        hop = lax.rem(owners[g] - me + replicas, replicas)
        start = (hop * CAP + position) * GROUP_ROWS
        target = jnp.where(mine, start + lane_slot, target)
        tags = jnp.where(row_group == g, slot[g].astype(F32), tags)
    compact = (iota((LIVE_ROWS, rows), 0) == packed).astype(BF16)
    spread = (iota((out_rows, rows), 0) == target).astype(BF16)
    pick[...] = compact.astype(F32).T.astype(BF16)
    place[...] = dot_cols(compact, spread).astype(BF16)
    compact_x[...] = dot(compact, x[...]).astype(BF16)
    sent[:, :feat] = dot(spread, x[...]).astype(BF16)
    sent[:, feat:] = dot(spread, tags.astype(BF16)).astype(BF16)


def prepare(owner, slot, live, x, replicas):
    rows, feat = x.shape
    out_rows = replicas * CAP * GROUP_ROWS
    smalls = [pltpu.SMEM(a.shape, jnp.int32) for a in (owner, slot, live)]
    return pl.pallas_call(
        functools.partial(prepare_kernel, replicas),
        out_shape=(
            jax.ShapeDtypeStruct((LIVE_ROWS, feat), BF16),
            jax.ShapeDtypeStruct((out_rows, feat + TAG), BF16),
            jax.ShapeDtypeStruct((rows, LIVE_ROWS), BF16),
            jax.ShapeDtypeStruct((LIVE_ROWS, out_rows), BF16),
        ),
        in_specs=[ANY, ANY, ANY, VMEM],
        out_specs=(VMEM,) * 4,
        scratch_shapes=smalls + [pltpu.SemaphoreType.DMA((3,))],
        compiler_params=params(60),
        name="prepare",
    )(owner, slot, live, x)


def first_kernel(at, x, w, out):
    out[...] = dot(x[...], w[...]).astype(BF16)


def first_chunk(at, x, weight):
    feat, _ = weight.shape
    tiles = CHUNK // TILE
    return pl.pallas_call(
        first_kernel,
        out_shape=jax.ShapeDtypeStruct((LIVE_ROWS, CHUNK), BF16),
        grid_spec=pltpu.PrefetchScalarGridSpec(
            num_scalar_prefetch=1,
            grid=(tiles,),
            in_specs=[
                pl.BlockSpec((LIVE_ROWS, feat), lambda i, at: (0, 0)),
                pl.BlockSpec((feat, TILE), lambda i, at: (0, at[0] * tiles + i)),
            ],
            out_specs=pl.BlockSpec((LIVE_ROWS, TILE), lambda i, at: (0, i)),
        ),
        compiler_params=params(),
        cost_estimate=cost(2 * LIVE_ROWS * feat * CHUNK, (feat + LIVE_ROWS) * CHUNK),
        name="first",
    )(at, x, weight)


def base_kernel(x, w, token_in, out, token):
    wide = dot(x[...], w[...]).astype(BF16)
    for j in range(out.shape[0]):
        out[j] = wide[:, j * CHUNK : (j + 1) * CHUNK]


def base_chunks(x, weight, token, group=2):
    feat, width = weight.shape
    number = width // CHUNK
    return pl.pallas_call(
        base_kernel,
        out_shape=(
            jax.ShapeDtypeStruct((number, LIVE_ROWS, CHUNK), BF16),
            jax.ShapeDtypeStruct(token.shape, token.dtype),
        ),
        grid=(number // group,),
        in_specs=[
            pl.BlockSpec((LIVE_ROWS, feat), lambda i: (0, 0)),
            pl.BlockSpec((feat, group * CHUNK), lambda i: (0, i)),
            ANY,
        ],
        out_specs=(pl.BlockSpec((group, LIVE_ROWS, CHUNK), lambda i: (i, 0, 0)), ANY),
        input_output_aliases={2: 1},
        compiler_params=params(),
        cost_estimate=cost(2 * LIVE_ROWS * feat * width, (feat + LIVE_ROWS) * width),
        name="base",
    )(x, weight, token)


def hop_kernel(at, base, *refs):
    out = refs[-2]
    total = base[0].astype(F32)
    if len(refs) == 4:
        total = total + refs[0][...].astype(F32)
    out[...] = total.astype(BF16)


def hop(chunk, base, got, token):
    here = pl.BlockSpec((LIVE_ROWS, TILE), lambda i, at: (0, i))
    inputs = [base] + ([got] if got is not None else []) + [token]
    return pl.pallas_call(
        hop_kernel,
        out_shape=(
            jax.ShapeDtypeStruct((LIVE_ROWS, CHUNK), BF16),
            jax.ShapeDtypeStruct(token.shape, token.dtype),
        ),
        grid_spec=pltpu.PrefetchScalarGridSpec(
            num_scalar_prefetch=1,
            grid=(CHUNK // TILE,),
            in_specs=[pl.BlockSpec((1, LIVE_ROWS, TILE), lambda i, at: (at[0], 0, i))]
            + [here] * (len(inputs) - 2)
            + [ANY],
            out_specs=(here, ANY),
        ),
        input_output_aliases={len(inputs): 1},
        compiler_params=params(),
        cost_estimate=cost(2 * LIVE_ROWS * CHUNK, 3 * LIVE_ROWS * CHUNK),
        name="hop",
    )(chunk.reshape(1), *inputs)


def fold(rank, adapters, half):
    shape = (adapters * rank, 2 * rank)
    return (iota(shape, 0) % rank + half * rank == iota(shape, 1)).astype(BF16)


def slot_mask(tag, rank, adapters):
    shape = (tag.shape[0], adapters * rank)
    return (iota(shape, 1) // rank).astype(F32) == tag.astype(F32)


def low_kernel(rank, blocks, down, *refs):
    parts, low = refs[:blocks], refs[blocks + 1]
    adapters = down.shape[0] // rank
    feat = down.shape[1]
    rows = parts[0].shape[0]
    half = blocks // 2
    maps = down[...]
    folds = [fold(rank, adapters, h) for h in range(2)]
    for k in range(half):
        total = None
        for h in range(2):
            part = parts[h * half + k]
            wide = dot_cols(part[:, :feat], maps)
            kept = jnp.where(slot_mask(part[:, feat : feat + 1], rank, adapters), wide, 0.0)
            got = dot(kept.astype(BF16), folds[h])
            total = got if total is None else total + got
        low[k * rows : (k + 1) * rows, :] = total.astype(BF16)


def low_values(parts, down, rank, token):
    rows, width = parts[0].shape
    blocks = len(parts)
    return pl.pallas_call(
        functools.partial(low_kernel, rank, blocks),
        out_shape=(
            jax.ShapeDtypeStruct((blocks // 2 * rows, 2 * rank), BF16),
            jax.ShapeDtypeStruct(token.shape, token.dtype),
        ),
        in_specs=[VMEM] * (blocks + 1) + [ANY],
        out_specs=(VMEM, ANY),
        input_output_aliases={blocks + 1: 1},
        compiler_params=params(),
        name="low",
    )(down, *parts, token)


def delta_kernel(rank, blocks, sums, up, *refs):
    tags, lows, outs = refs[:blocks], refs[blocks : blocks + sums], refs[blocks + sums + 1 :]
    adapters = up.shape[0] // rank
    rows = tags[0].shape[0]
    half = blocks // 2
    total = lows[0][...].astype(F32)
    for other in lows[1:]:
        total = total + other[...].astype(F32)
    low = total.astype(BF16)
    maps = up[...]
    for h in range(2):
        spread = fold(rank, adapters, h)
        for k in range(half):
            wide = dot_cols(low[k * rows : (k + 1) * rows, :], spread)
            mask = slot_mask(tags[h * half + k][:, :1], rank, adapters)
            kept = jnp.where(mask, wide, 0.0).astype(BF16)
            outs[h * half + k][...] = dot(kept, maps).astype(BF16)


def delta_values(parts, lows, up, rank, token):
    rows, width = parts[0].shape
    blocks = len(parts)
    columns = up.shape[1]
    tag = pl.BlockSpec((rows, TAG), lambda i: (0, width // TAG - 1))
    whole = lambda a: pl.BlockSpec(a.shape, lambda i: (0, 0))
    return pl.pallas_call(
        functools.partial(delta_kernel, rank, blocks, len(lows)),
        out_shape=[jax.ShapeDtypeStruct((rows, columns), BF16)] * blocks
        + [jax.ShapeDtypeStruct(token.shape, token.dtype)],
        grid=(1,),
        in_specs=[whole(up)] + [tag] * blocks + [whole(a) for a in lows] + [ANY],
        out_specs=[pl.BlockSpec((rows, columns), lambda i: (0, 0))] * blocks + [ANY],
        input_output_aliases={1 + blocks + len(lows): blocks},
        compiler_params=params(),
        name="delta",
    )(up, *parts, *lows, token)


def add_delta_kernel(blocks, at, base, place, *refs):
    parts, out = refs[:blocks], refs[blocks + 1]
    rows = parts[0].shape[0]
    total = base[0].astype(F32)
    for k in range(blocks):
        total = total + dot(place[:, k * rows : (k + 1) * rows], parts[k][...])
    out[0] = total.astype(BF16)


def add_delta(first, base, place, parts, token):
    rows, columns = parts[0].shape
    chunk = base.shape[2]
    here = pl.BlockSpec((1, LIVE_ROWS, chunk), lambda i, at: (at[0] + i, 0, 0))
    return pl.pallas_call(
        functools.partial(add_delta_kernel, len(parts)),
        out_shape=(
            jax.ShapeDtypeStruct(base.shape, base.dtype),
            jax.ShapeDtypeStruct(token.shape, token.dtype),
        ),
        grid_spec=pltpu.PrefetchScalarGridSpec(
            num_scalar_prefetch=1,
            grid=(columns // chunk,),
            in_specs=[here, pl.BlockSpec(place.shape, lambda i, at: (0, 0))]
            + [pl.BlockSpec((rows, chunk), lambda i, at: (0, i))] * len(parts)
            + [ANY],
            out_specs=(here, ANY),
        ),
        input_output_aliases={1: 0, 3 + len(parts): 1},
        compiler_params=params(),
        name="add_delta",
    )(first, base, place, *parts, token)


def finish_kernel(at, base, left, right, pick, *refs):
    out, _, made, sems = refs[-4:]
    tile, tiles = pl.program_id(0), pl.num_programs(0)

    def copy(i):
        column = pl.multiple_of(at[0] * CHUNK + i * TILE, TILE)
        return pltpu.make_async_copy(made.at[i], out.at[:, pl.ds(column, TILE)], sems.at[i])

    @pl.when(at[1] > 0)
    def _():
        total = base[0].astype(F32) + left[...].astype(F32) + right[...].astype(F32)
        made[tile] = dot(pick[...], total.astype(BF16)).astype(BF16)
        copy(tile).start()

        @pl.when(tile == tiles - 1)
        def _():
            for i in range(CHUNK // TILE):
                copy(i).wait()


def finish(at, base, left, right, pick, held, token):
    rows, width = pick.shape[0], base.shape[0] * CHUNK
    tiles = CHUNK // TILE
    got = pl.BlockSpec((LIVE_ROWS, TILE), lambda i, at: (0, i))
    last = [token] if held is None else [held, token]
    aliases = {6: 1} if held is not None else {5: 1}
    if held is not None:
        aliases[5] = 0
    return pl.pallas_call(
        finish_kernel,
        out_shape=(
            jax.ShapeDtypeStruct((rows, width), BF16),
            jax.ShapeDtypeStruct(token.shape, token.dtype),
        ),
        grid_spec=pltpu.PrefetchScalarGridSpec(
            num_scalar_prefetch=1,
            grid=(tiles,),
            in_specs=[
                pl.BlockSpec((1, LIVE_ROWS, TILE), lambda i, at: (at[0], 0, i)),
                got,
                got,
                pl.BlockSpec(pick.shape, lambda i, at: (0, 0)),
            ]
            + [ANY] * len(last),
            out_specs=(ANY, ANY),
            scratch_shapes=[pltpu.VMEM((tiles, rows, TILE), BF16), pltpu.SemaphoreType.DMA((tiles,))],
        ),
        input_output_aliases=aliases,
        compiler_params=params(),
        cost_estimate=cost(2 * LIVE_ROWS * rows * CHUNK, 6 * LIVE_ROWS * CHUNK),
        name="finish",
    )(at, base, left, right, pick, *last)


def send_groups(sent):
    replicas = lax.axis_size("replica")
    rows = CAP * GROUP_ROWS
    parts = [sent[:rows]]
    for k in range(1, replicas):
        hops = [(i, (i + k) % replicas) for i in range(replicas)]
        parts.append(lax.ppermute(sent[k * rows : (k + 1) * rows], "replica", hops))
    return parts


def send_lows(low):
    shards = lax.axis_size("tensor")
    if shards > 4:
        return [lax.psum(low, "tensor")]
    lows = [low]
    for k in range(1, shards):
        hops = [(i, (i + k) % shards) for i in range(shards)]
        lows.append(lax.ppermute(low, "tensor", hops))
    return lows


def send_back(made):
    replicas = lax.axis_size("replica")
    back = [made[0]]
    for k in range(1, replicas):
        hops = [(i, (i - k) % replicas) for i in range(replicas)]
        back.append(lax.ppermute(made[k], "replica", hops))
    return back


def on_device(x, owner, slot, live, weight, down, up):
    rows = x.shape[0]
    width = weight.shape[1]
    rank = down.shape[1]
    replicas, shards = lax.axis_size("replica"), lax.axis_size("tensor")
    z = lax.axis_index("tensor").astype(jnp.int32)
    compact_x, sent, pick, place = prepare(owner[:, 0], slot, live[0], x, replicas)
    share = width // shards
    down, up = down.reshape(-1, down.shape[2]), up.reshape(-1, up.shape[2])
    token = jnp.zeros((8, 128), jnp.int32)
    if shards != 4:
        base = dot(compact_x, weight)
        parts = send_groups(sent)
        low, token = low_values(parts, down, rank, token)
        *made, token = delta_values(parts, send_lows(low), up, rank, token)
        back = jnp.concatenate(send_back(made), axis=0)
        mine = lax.dynamic_slice_in_dim(base, z * share, share, 1) + dot(place, back)
        base = lax.dynamic_update_slice_in_dim(base, mine, z * share, 1).astype(BF16)
        total = lax.psum_scatter(base, "tensor", scatter_dimension=1, tiled=True)
        total = lax.all_gather(total, "tensor", axis=1, tiled=True)
        return dot(pick, total).astype(BF16)

    chunks, per = width // CHUNK, share // CHUNK
    inner = (z == 1) | (z == 2)
    even_right, odd_right = z % 2 == 0, z % 2 == 1
    even = [(0, 1), (1, 0), (2, 3), (3, 2)]
    odd = [(1, 2), (2, 1)]

    def chunk_of(position, right):
        return jnp.clip(jnp.where(right, chunks - 1 - position, position), 0, chunks - 1)

    def even_chunk(step):
        return chunk_of(step - jnp.where(inner, 3, 0), even_right)

    def odd_chunk(step):
        return chunk_of(jnp.int32(step - 1), odd_right)

    evens, odds = {}, {}
    result = None
    message = first_chunk(even_chunk(0).reshape(1), compact_x, weight)
    evens[0] = lax.ppermute(message, "tensor", even)
    parts = send_groups(sent)
    base, token = base_chunks(compact_x, weight, token)
    low, token = low_values(parts, down, rank, token)
    lows = send_lows(low)
    unfinished = list(range(chunks + 3))
    seen_even, seen_odd = set(), set()

    def close(result, token, base):
        for a in list(unfinished):
            b = chunks - a
            if a not in seen_even or (1 <= b <= chunks and b not in seen_odd):
                continue
            unfinished.remove(a)
            position = jnp.where(inner, a, a - 3)
            valid = (position >= 0) & (position < chunks)
            at = jnp.stack([chunk_of(position, ~even_right), valid.astype(jnp.int32)])
            other = odds[b] if 1 <= b <= chunks else odds[1]
            result, token = finish(at, base, evens[a], other, pick, result, token)
        return result, token

    for step in range(1, chunks + 3):
        message, token = hop(even_chunk(step), base, odds.get(step - 2), token)
        evens[step] = lax.ppermute(message, "tensor", even)
        seen_odd.add(step - 2)
        if step == 2:
            *made, token = delta_values(parts, lows, up, rank, token)
            back = send_back(made)
        if step == 3 + per - 1:
            base, token = add_delta((z * per).reshape(1), base, place, back, token)
        result, token = close(result, token, base)
        if step <= chunks:
            message, token = hop(odd_chunk(step), base, evens[step - 1], token)
            odds[step] = lax.ppermute(message, "tensor", odd)
        seen_even.add(step - 1)
        result, token = close(result, token, base)
    seen_even.add(chunks + 2)
    result, token = close(result, token, base)
    return result


def solution(mesh):
    placed = (
        P(("parts", "replica"), "tensor"),
        P(("parts", "replica"), None),
        P(("parts", "replica")),
        P(("parts", "replica"), None),
        P("tensor", None),
        P("replica", None, "tensor"),
        P("replica", None, "tensor"),
    )
    return jax.shard_map(
        on_device,
        mesh=mesh,
        in_specs=placed,
        out_specs=P(("parts", "replica"), None),
        check_vma=False,
    )
```

```python
import functools

import jax
import jax.numpy as jnp
from jax import lax
from jax.experimental import pallas as pl
from jax.experimental.pallas import tpu as pltpu
from jax.sharding import PartitionSpec as P

GROUP_ROWS = 16
CAP = 4
LIVE_ROWS = 224
TAG = 128
CHUNK = 1024
TILE = 512
BF16 = jnp.bfloat16
F32 = jnp.float32
MIB = 1024 * 1024
PREPARE_MIB = 60
DELTA_AT = 2


def dot(a, b):
    return jnp.dot(a, b, preferred_element_type=F32)


def dot_cols(a, b):
    return lax.dot_general(a, b, (((1,), (1,)), ((), ())), preferred_element_type=F32)


def iota(shape, dim):
    return lax.broadcasted_iota(jnp.int32, shape, dim)


def params(mib=50):
    return pltpu.CompilerParams(vmem_limit_bytes=mib * MIB)


def cost(flops, elements):
    return pl.CostEstimate(flops=flops, bytes_accessed=2 * elements, transcendentals=0)


ANY = pl.BlockSpec(memory_space=pl.ANY)
VMEM = pl.BlockSpec(memory_space=pltpu.VMEM)


def is_inner():
    z = lax.axis_index("tensor")
    return (z == 1) | (z == 2)


def chunk_at(q, chunks):
    return jnp.where(lax.axis_index("tensor") % 2 == 0, chunks - 1 - q, q)


def weight_copy(w, q, into, sem):
    column = pl.multiple_of(chunk_at(q, w.shape[1] // CHUNK) * CHUNK, CHUNK)
    return pltpu.make_async_copy(w.at[:, pl.ds(column, CHUNK)], into, sem)


def prepare_kernel(replicas, line, owner_in, slot_in, live_in, x_in, *refs):
    refs = list(refs)
    w = refs.pop(0) if line else None
    compact_x, pick, place = refs[:3]
    blocks = refs[3 : 3 + replicas]
    message = refs[3 + replicas] if line else None
    owner, slot, live, x, sems = refs[-5:]
    wide, wide_sem = (refs[-7], refs[-6]) if line else (None, None)
    copies = [
        pltpu.make_async_copy(src, dst, sems.at[i])
        for i, (src, dst) in enumerate(((owner_in, owner), (slot_in, slot), (live_in, live), (x_in, x)))
    ]
    for copy in copies:
        copy.start()
    if line:
        weights = weight_copy(w, 0, wide, wide_sem.at[0])
        weights.start()
    for copy in copies:
        copy.wait()
    me = lax.axis_index("replica")
    rows, feat = x.shape
    groups = rows // GROUP_ROWS
    out_rows = replicas * CAP * GROUP_ROWS
    lane = iota((1, rows), 1)
    lane_group, lane_slot = lane // GROUP_ROWS, lane % GROUP_ROWS
    row_group = iota((rows, TAG), 0) // GROUP_ROWS
    packed = jnp.full((1, rows), -1, jnp.int32)
    target = jnp.zeros((1, rows), jnp.int32)
    tags = jnp.zeros((rows, TAG), F32)
    owners = [owner[g] for g in range(groups)]
    offset = jnp.int32(0)
    used = [jnp.int32(0)] * replicas
    for g in range(groups):
        count = live[g]
        mine = lane_group == g
        packed = jnp.where(mine & (lane_slot < count), offset + lane_slot, packed)
        offset = offset + count
        position = jnp.int32(0)
        for o in range(replicas):
            hit = owners[g] == o
            position = jnp.where(hit, used[o], position)
            used[o] = used[o] + hit.astype(jnp.int32)
        hop = lax.rem(owners[g] - me + replicas, replicas)
        start = (hop * CAP + position) * GROUP_ROWS
        target = jnp.where(mine, start + lane_slot, target)
        tags = jnp.where(row_group == g, slot[g].astype(F32), tags)
    compact = (iota((LIVE_ROWS, rows), 0) == packed).astype(BF16)
    spread = (iota((out_rows, rows), 0) == target).astype(BF16)
    pick[...] = compact.astype(F32).T.astype(BF16)
    place[...] = dot_cols(compact, spread).astype(BF16)
    packed_x = dot(compact, x[...]).astype(BF16)
    compact_x[...] = packed_x
    sent = dot(spread, x[...]).astype(BF16)
    sent_tags = dot(spread, tags.astype(BF16)).astype(BF16)
    for k, block in enumerate(blocks):
        here = slice(k * block.shape[0], (k + 1) * block.shape[0])
        block[:, :feat] = sent[here]
        block[:, feat:] = sent_tags[here]
    if line:
        weights.wait()
        message[...] = dot(packed_x, wide[...]).astype(BF16)


def prepare(owner, slot, live, x, replicas, weight=None):
    rows, feat = x.shape
    block = CAP * GROUP_ROWS
    line = weight is not None
    shape = lambda *dims: jax.ShapeDtypeStruct(dims, BF16)
    outs = [shape(LIVE_ROWS, feat), shape(rows, LIVE_ROWS), shape(LIVE_ROWS, replicas * block)]
    outs += [shape(block, feat + TAG)] * replicas
    scratch = [pltpu.SMEM(a.shape, jnp.int32) for a in (owner, slot, live)]
    scratch += [pltpu.VMEM(x.shape, BF16), pltpu.SemaphoreType.DMA((4,))]
    if line:
        outs.append(shape(LIVE_ROWS, CHUNK))
        scratch = [pltpu.VMEM((feat, CHUNK), BF16), pltpu.SemaphoreType.DMA((1,))] + scratch
    return pl.pallas_call(
        functools.partial(prepare_kernel, replicas, line),
        out_shape=outs,
        in_specs=[ANY] * (5 if line else 4),
        out_specs=[VMEM] * len(outs),
        scratch_shapes=scratch,
        compiler_params=params(PREPARE_MIB),
        name="prepare",
    )(owner, slot, live, x, *([weight] if line else []))


def base_kernel(places, x, w, token_in, *refs):
    outs, wide, sems = refs[: len(places)], refs[-2], refs[-1]
    slots = wide.shape[0]
    copies = [weight_copy(w, q, wide.at[i % slots], sems.at[i % slots]) for i, q in enumerate(places)]
    for copy in copies[: slots - 1]:
        copy.start()
    for i, copy in enumerate(copies):
        if i + slots - 1 < len(copies):
            copies[i + slots - 1].start()
        copy.wait()
        outs[i][...] = dot(x[...], wide[i % slots]).astype(BF16)


def base_chunks(places, x, weight, token):
    feat, _ = weight.shape
    elements = (feat + LIVE_ROWS) * CHUNK * len(places)
    return pl.pallas_call(
        functools.partial(base_kernel, places),
        out_shape=[jax.ShapeDtypeStruct((LIVE_ROWS, CHUNK), BF16)] * len(places)
        + [jax.ShapeDtypeStruct(token.shape, token.dtype)],
        in_specs=[VMEM, ANY, ANY],
        out_specs=[VMEM] * len(places) + [ANY],
        input_output_aliases={2: len(places)},
        scratch_shapes=[pltpu.VMEM((3, feat, CHUNK), BF16), pltpu.SemaphoreType.DMA((3,))],
        compiler_params=params(),
        cost_estimate=cost(2 * feat * LIVE_ROWS * CHUNK * len(places), elements),
        name="base",
    )(x, weight, token)


def odd_hop_kernel(base, got, token_in, out, token):
    out[...] = (base[...].astype(F32) + got[...].astype(F32)).astype(BF16)


def even_hop_kernel(near, far, got, token_in, out, token):
    @pl.when(is_inner())
    def _():
        out[...] = (near[...].astype(F32) + got[...].astype(F32)).astype(BF16)

    @pl.when(jnp.logical_not(is_inner()))
    def _():
        out[...] = far[...]


def hop(kernel, inputs, token):
    return pl.pallas_call(
        kernel,
        out_shape=(
            jax.ShapeDtypeStruct((LIVE_ROWS, CHUNK), BF16),
            jax.ShapeDtypeStruct(token.shape, token.dtype),
        ),
        in_specs=[VMEM] * len(inputs) + [ANY],
        out_specs=(VMEM, ANY),
        input_output_aliases={len(inputs): 1},
        compiler_params=params(),
        cost_estimate=cost(2 * LIVE_ROWS * CHUNK, 3 * LIVE_ROWS * CHUNK),
        name="hop",
    )(*inputs, token)


def fold(rank, adapters, half):
    shape = (adapters * rank, 2 * rank)
    return (iota(shape, 0) % rank + half * rank == iota(shape, 1)).astype(BF16)


def slot_mask(tag, rank, adapters):
    shape = (tag.shape[0], adapters * rank)
    return (iota(shape, 1) // rank).astype(F32) == tag.astype(F32)


def low_kernel(rank, blocks, down, *refs):
    parts, low = refs[:blocks], refs[blocks + 1]
    adapters = down.shape[0] // rank
    feat = down.shape[1]
    rows = parts[0].shape[0]
    half = blocks // 2
    maps = down[...]
    folds = [fold(rank, adapters, h) for h in range(2)]
    for k in range(half):
        total = None
        for h in range(2):
            part = parts[h * half + k]
            wide = dot_cols(part[:, :feat], maps)
            kept = jnp.where(slot_mask(part[:, feat : feat + 1], rank, adapters), wide, 0.0)
            got = dot(kept.astype(BF16), folds[h])
            total = got if total is None else total + got
        low[k * rows : (k + 1) * rows, :] = total.astype(BF16)


def low_values(parts, down, rank, token):
    rows, width = parts[0].shape
    blocks = len(parts)
    return pl.pallas_call(
        functools.partial(low_kernel, rank, blocks),
        out_shape=(
            jax.ShapeDtypeStruct((blocks // 2 * rows, 2 * rank), BF16),
            jax.ShapeDtypeStruct(token.shape, token.dtype),
        ),
        in_specs=[VMEM] * (blocks + 1) + [ANY],
        out_specs=(VMEM, ANY),
        input_output_aliases={blocks + 1: 1},
        compiler_params=params(),
        name="low",
    )(down, *parts, token)


def delta_kernel(rank, blocks, sums, up, *refs):
    tags, lows, outs = refs[:blocks], refs[blocks : blocks + sums], refs[blocks + sums + 1 :]
    adapters = up.shape[0] // rank
    rows = tags[0].shape[0]
    half = blocks // 2
    total = lows[0][...].astype(F32)
    for other in lows[1:]:
        total = total + other[...].astype(F32)
    low = total.astype(BF16)
    maps = up[...]
    for h in range(2):
        spread = fold(rank, adapters, h)
        for k in range(half):
            wide = dot_cols(low[k * rows : (k + 1) * rows, :], spread)
            mask = slot_mask(tags[h * half + k][:, :1], rank, adapters)
            kept = jnp.where(mask, wide, 0.0).astype(BF16)
            outs[h * half + k][...] = dot(kept, maps).astype(BF16)


def delta_values(parts, lows, up, rank, token):
    rows, width = parts[0].shape
    blocks = len(parts)
    columns = up.shape[1]
    tag = pl.BlockSpec((rows, TAG), lambda i: (0, width // TAG - 1))
    whole = lambda a: pl.BlockSpec(a.shape, lambda i: (0, 0))
    return pl.pallas_call(
        functools.partial(delta_kernel, rank, blocks, len(lows)),
        out_shape=[jax.ShapeDtypeStruct((rows, columns), BF16)] * blocks
        + [jax.ShapeDtypeStruct(token.shape, token.dtype)],
        grid=(1,),
        in_specs=[whole(up)] + [tag] * blocks + [whole(a) for a in lows] + [ANY],
        out_specs=[pl.BlockSpec((rows, columns), lambda i: (0, 0))] * blocks + [ANY],
        input_output_aliases={1 + blocks + len(lows): blocks},
        compiler_params=params(),
        name="delta",
    )(up, *parts, *lows, token)


def add_delta_kernel(per, chunks, place, *refs):
    bases, refs = refs[: 2 * per], refs[2 * per :]
    outs, parts = refs[-2 * per - 1 : -1], refs[: -2 * per - 2]
    rows = parts[0].shape[0]
    inner = is_inner()
    z = lax.axis_index("tensor")
    for j in range(per):
        chunk = chunk_at(jnp.where(inner, per, 3 * per) + j, chunks)
        column = pl.multiple_of((chunk - z * per) * CHUNK, CHUNK)
        total = None
        for k, part in enumerate(parts):
            got = dot(place[:, k * rows : (k + 1) * rows], part[:, pl.ds(column, CHUNK)])
            total = got if total is None else total + got
        for i, mine in ((j, inner), (per + j, jnp.logical_not(inner))):
            wide = bases[i][...].astype(F32)
            outs[i][...] = (wide + jnp.where(mine, total, 0.0)).astype(BF16)


def add_delta(bases, place, parts, chunks, token):
    per = len(bases) // 2
    inputs = [place, *bases, *parts]
    return pl.pallas_call(
        functools.partial(add_delta_kernel, per, chunks),
        out_shape=[jax.ShapeDtypeStruct(bases[0].shape, BF16)] * len(bases)
        + [jax.ShapeDtypeStruct(token.shape, token.dtype)],
        in_specs=[VMEM] * len(inputs) + [ANY],
        out_specs=[VMEM] * len(bases) + [ANY],
        input_output_aliases={len(inputs): len(bases)},
        compiler_params=params(),
        name="add_delta",
    )(*inputs, token)


def finish_kernel(chunks, near_q, far_q, *refs):
    refs = list(refs)
    near = refs.pop(0) if near_q is not None else None
    far = refs.pop(0) if far_q is not None else None
    even, odd = refs.pop(0), refs.pop(0) if near_q is not None else None
    pick = refs.pop(0)
    out, _, made, sems = refs[-4:]
    tiles = CHUNK // TILE

    def write(q, terms):
        column = chunk_at(q, chunks) * CHUNK
        copies = []
        for i in range(tiles):
            total = sum(term[:, i * TILE : (i + 1) * TILE].astype(F32) for term in terms)
            made[i] = dot(pick[...], total.astype(BF16)).astype(BF16)
            here = pl.ds(pl.multiple_of(column + i * TILE, TILE), TILE)
            copies.append(pltpu.make_async_copy(made.at[i], out.at[:, here], sems.at[i]))
            copies[-1].start()
        for copy in copies:
            copy.wait()

    if near_q is not None:

        @pl.when(is_inner())
        def _():
            write(near_q, [near, even, odd])

    if far_q is not None:

        @pl.when(jnp.logical_not(is_inner()))
        def _():
            write(far_q, [far, even])


def finish(near_q, far_q, bases, even, odd, pick, held, token):
    rows, chunks = pick.shape[0], len(bases)
    inputs = [bases[q] for q in (near_q, far_q) if q is not None] + [even]
    inputs += [odd] if near_q is not None else []
    inputs += [pick]
    last = [token] if held is None else [held, token]
    aliases = {len(inputs) + len(last) - 1: 1}
    if held is not None:
        aliases[len(inputs)] = 0
    return pl.pallas_call(
        functools.partial(finish_kernel, chunks, near_q, far_q),
        out_shape=(
            jax.ShapeDtypeStruct((rows, chunks * CHUNK), BF16),
            jax.ShapeDtypeStruct(token.shape, token.dtype),
        ),
        in_specs=[VMEM] * len(inputs) + [ANY] * len(last),
        out_specs=(ANY, ANY),
        scratch_shapes=[pltpu.VMEM((CHUNK // TILE, rows, TILE), BF16), pltpu.SemaphoreType.DMA((CHUNK // TILE,))],
        input_output_aliases=aliases,
        compiler_params=params(),
        cost_estimate=cost(2 * LIVE_ROWS * rows * CHUNK, 6 * LIVE_ROWS * CHUNK),
        name="finish",
    )(*inputs, *last)


def send_groups(blocks):
    replicas = lax.axis_size("replica")
    parts = [blocks[0]]
    for k in range(1, replicas):
        hops = [(i, (i + k) % replicas) for i in range(replicas)]
        parts.append(lax.ppermute(blocks[k], "replica", hops))
    return parts


def send_lows(low):
    shards = lax.axis_size("tensor")
    if shards > 4:
        return [lax.psum(low, "tensor")]
    lows = [low]
    for k in range(1, shards):
        hops = [(i, (i + k) % shards) for i in range(shards)]
        lows.append(lax.ppermute(low, "tensor", hops))
    return lows


def send_back(made):
    replicas = lax.axis_size("replica")
    back = [made[0]]
    for k in range(1, replicas):
        hops = [(i, (i - k) % replicas) for i in range(replicas)]
        back.append(lax.ppermute(made[k], "replica", hops))
    return back


def on_device(x, owner, slot, live, weight, down, up):
    width = weight.shape[1]
    rank = down.shape[1]
    replicas, shards = lax.axis_size("replica"), lax.axis_size("tensor")
    share = width // shards
    down, up = down.reshape(-1, down.shape[2]), up.reshape(-1, up.shape[2])
    token = jnp.zeros((8, 128), jnp.int32)
    if shards != 4:
        compact_x, pick, place, *blocks = prepare(owner[:, 0], slot, live[0], x, replicas)
        z = lax.axis_index("tensor").astype(jnp.int32)
        base = dot(compact_x, weight)
        parts = send_groups(blocks)
        low, token = low_values(parts, down, rank, token)
        *made, token = delta_values(parts, send_lows(low), up, rank, token)
        back = jnp.concatenate(send_back(made), axis=0)
        mine = lax.dynamic_slice_in_dim(base, z * share, share, 1) + dot(place, back)
        base = lax.dynamic_update_slice_in_dim(base, mine, z * share, 1).astype(BF16)
        total = lax.psum_scatter(base, "tensor", scatter_dimension=1, tiled=True)
        total = lax.all_gather(total, "tensor", axis=1, tiled=True)
        return dot(pick, total).astype(BF16)

    chunks, per = width // CHUNK, share // CHUNK
    even = [(0, 1), (1, 0), (2, 3), (3, 2)]
    odd = [(1, 2), (2, 1)]
    compact_x, pick, place, *rest = prepare(owner[:, 0], slot, live[0], x, replicas, weight)
    blocks, message = rest[:-1], rest[-1]
    evens, odds = {0: lax.ppermute(message, "tensor", even)}, {}
    parts = send_groups(blocks)
    *early, token = base_chunks((1, 2), compact_x, weight, token)
    bases = [message, *early]
    for step in (1, 2):
        evens[step] = lax.ppermute(bases[step], "tensor", even)
    *late, token = base_chunks(tuple(range(3, chunks)), compact_x, weight, token)
    bases += late
    low, token = low_values(parts, down, rank, token)
    lows = send_lows(low)
    steps = chunks + 3
    result = None
    unfinished = list(range(steps))
    seen_even, seen_odd = set(), set()

    def close(result, token):
        for a in list(unfinished):
            b = chunks - a
            if a not in seen_even or (1 <= b <= chunks and b not in seen_odd):
                continue
            unfinished.remove(a)
            near_q = chunks - 1 - a if a < chunks else None
            far_q = chunks + 2 - a if a >= 3 else None
            result, token = finish(near_q, far_q, bases, evens[a], odds.get(b), pick, result, token)
        return result, token

    for step in range(1, steps):
        if step >= 3:
            far = bases[min(step, chunks - 1)]
            inputs = [bases[step - 3], far, odds[step - 2]]
            message, token = hop(even_hop_kernel, inputs, token)
            evens[step] = lax.ppermute(message, "tensor", even)
            seen_odd.add(step - 2)
            result, token = close(result, token)
        if step <= chunks:
            message, token = hop(odd_hop_kernel, [bases[chunks - step], evens[step - 1]], token)
            odds[step] = lax.ppermute(message, "tensor", odd)
        seen_even.add(step - 1)
        if step == DELTA_AT:
            *made, token = delta_values(parts, lows, up, rank, token)
            back = send_back(made)
        if step == per + 2:
            own = list(range(per, 2 * per)) + list(range(3 * per, 4 * per))
            *summed, token = add_delta([bases[q] for q in own], place, back, chunks, token)
            for q, value in zip(own, summed):
                bases[q] = value
        result, token = close(result, token)
    seen_even.add(steps - 1)
    result, token = close(result, token)
    return result


def solution(mesh):
    placed = (
        P(("parts", "replica"), "tensor"),
        P(("parts", "replica"), None),
        P(("parts", "replica")),
        P(("parts", "replica"), None),
        P("tensor", None),
        P("replica", None, "tensor"),
        P("replica", None, "tensor"),
    )
    return jax.shard_map(
        on_device,
        mesh=mesh,
        in_specs=placed,
        out_specs=P(("parts", "replica"), None),
        check_vma=False,
    )
```

```python
import functools

import jax
import jax.numpy as jnp
from jax import lax
from jax.experimental import pallas as pl
from jax.experimental.pallas import tpu as pltpu
from jax.sharding import PartitionSpec as P

GROUP_ROWS = 16
CAP = 4
LIVE_ROWS = 224
TAG = 128
LANES = 128
CUTS = 3
BF16 = jnp.bfloat16
F32 = jnp.float32
MIB = 1024 * 1024
HOP_WORK = 14000
FIRST_HOP_WORK = 8000
BASE_WORK = 400000
PREPARE_MIB = 60
DELTA_AT = 1


def dot(a, b):
    return jnp.dot(a, b, preferred_element_type=F32)


def dot_cols(a, b):
    return lax.dot_general(a, b, (((1,), (1,)), ((), ())), preferred_element_type=F32)


def iota(shape, dim):
    return lax.broadcasted_iota(jnp.int32, shape, dim)


def params(mib=50):
    return pltpu.CompilerParams(vmem_limit_bytes=mib * MIB)


def cost(flops, elements):
    return pl.CostEstimate(flops=flops, bytes_accessed=2 * elements, transcendentals=0)


ANY = pl.BlockSpec(memory_space=pl.ANY)
VMEM = pl.BlockSpec(memory_space=pltpu.VMEM)


def is_inner():
    z = lax.axis_index("tensor")
    return (z == 1) | (z == 2)


def widths_of(width, shards):
    tiles = width // shards // LANES
    if CUTS == 3:
        side = tiles // 3
        cuts = (side, tiles - 2 * side, side)
    else:
        cuts = (tiles // CUTS,) * CUTS
    return tuple(cut * LANES for cut in cuts) * shards


def column_at(q, widths):
    left, right = sum(widths[:q]), sum(widths[: len(widths) - 1 - q])
    column = jnp.where(lax.axis_index("tensor") % 2 == 0, right, left)
    return pl.multiple_of(column, LANES)


def weight_copy(w, q, widths, into, sem):
    return pltpu.make_async_copy(w.at[:, pl.ds(column_at(q, widths), widths[q])], into, sem)


def prepare_kernel(replicas, widths, owner_in, slot_in, live_in, x_in, *refs):
    refs = list(refs)
    line = widths is not None
    w = refs.pop(0) if line else None
    compact_x, pick, place, spread_out, tags_out = refs[:5]
    message = refs[5] if line else None
    owner, slot, live, x, sems = refs[-5:]
    wide, wide_sem = (refs[-7], refs[-6]) if line else (None, None)
    copies = [
        pltpu.make_async_copy(src, dst, sems.at[i])
        for i, (src, dst) in enumerate(((owner_in, owner), (slot_in, slot), (live_in, live), (x_in, x)))
    ]
    for copy in copies:
        copy.start()
    if line:
        weights = weight_copy(w, 0, widths, wide, wide_sem.at[0])
        weights.start()
    for copy in copies:
        copy.wait()
    me = lax.axis_index("replica")
    rows, feat = x.shape
    groups = rows // GROUP_ROWS
    out_rows = replicas * CAP * GROUP_ROWS
    lane = iota((1, rows), 1)
    lane_group, lane_slot = lane // GROUP_ROWS, lane % GROUP_ROWS
    row_group = iota((rows, TAG), 0) // GROUP_ROWS
    packed = jnp.full((1, rows), -1, jnp.int32)
    target = jnp.zeros((1, rows), jnp.int32)
    tags = jnp.zeros((rows, TAG), F32)
    owners = [owner[g] for g in range(groups)]
    offset = jnp.int32(0)
    used = [jnp.int32(0)] * replicas
    for g in range(groups):
        count = live[g]
        mine = lane_group == g
        packed = jnp.where(mine & (lane_slot < count), offset + lane_slot, packed)
        offset = offset + count
        position = jnp.int32(0)
        for o in range(replicas):
            hit = owners[g] == o
            position = jnp.where(hit, used[o], position)
            used[o] = used[o] + hit.astype(jnp.int32)
        hop = lax.rem(owners[g] - me + replicas, replicas)
        start = (hop * CAP + position) * GROUP_ROWS
        target = jnp.where(mine, start + lane_slot, target)
        tags = jnp.where(row_group == g, slot[g].astype(F32), tags)
    compact = (iota((LIVE_ROWS, rows), 0) == packed).astype(BF16)
    spread = (iota((out_rows, rows), 0) == target).astype(BF16)
    pick[...] = compact.astype(F32).T.astype(BF16)
    place[...] = dot_cols(compact, spread).astype(BF16)
    packed_x = dot(compact, x[...]).astype(BF16)
    compact_x[...] = packed_x
    spread_out[...] = spread
    tags_out[...] = tags.astype(BF16)
    if line:
        weights.wait()
        message[...] = dot(packed_x, wide[...]).astype(BF16)


def prepare(owner, slot, live, x, replicas, weight=None, widths=None):
    rows, feat = x.shape
    block = CAP * GROUP_ROWS
    line = weight is not None
    shape = lambda *dims: jax.ShapeDtypeStruct(dims, BF16)
    outs = [shape(LIVE_ROWS, feat), shape(rows, LIVE_ROWS), shape(LIVE_ROWS, replicas * block)]
    outs += [shape(replicas * block, rows), shape(rows, TAG)]
    scratch = [pltpu.SMEM(a.shape, jnp.int32) for a in (owner, slot, live)]
    scratch += [pltpu.VMEM(x.shape, BF16), pltpu.SemaphoreType.DMA((4,))]
    if line:
        outs.append(shape(LIVE_ROWS, widths[0]))
        scratch = [pltpu.VMEM((feat, widths[0]), BF16), pltpu.SemaphoreType.DMA((1,))] + scratch
    return pl.pallas_call(
        functools.partial(prepare_kernel, replicas, widths),
        out_shape=outs,
        in_specs=[ANY] * (5 if line else 4),
        out_specs=[VMEM] * len(outs),
        scratch_shapes=scratch,
        compiler_params=params(PREPARE_MIB),
        name="prepare",
    )(owner, slot, live, x, *([weight] if line else []))


def spread_kernel(spread, tags, x, token_in, *blocks):
    feat = x.shape[1]
    sent = dot(spread[...], x[...]).astype(BF16)
    sent_tags = dot(spread[...], tags[...]).astype(BF16)
    for k, block in enumerate(blocks[:-1]):
        here = slice(k * block.shape[0], (k + 1) * block.shape[0])
        block[:, :feat] = sent[here]
        block[:, feat:] = sent_tags[here]


def spread_groups(spread, tags, x, token):
    rows = CAP * GROUP_ROWS
    blocks = spread.shape[0] // rows
    return pl.pallas_call(
        spread_kernel,
        out_shape=[jax.ShapeDtypeStruct((rows, x.shape[1] + TAG), BF16)] * blocks
        + [jax.ShapeDtypeStruct(token.shape, token.dtype)],
        in_specs=[VMEM] * 3 + [ANY],
        out_specs=[VMEM] * blocks + [ANY],
        input_output_aliases={3: blocks},
        compiler_params=params(),
        name="spread",
    )(spread, tags, x, token)


def base_kernel(places, widths, x, w, token_in, *refs):
    outs, wide, sems = refs[: len(places)], refs[-2], refs[-1]
    slots = wide.shape[0]
    copies = [
        weight_copy(w, q, widths, wide.at[i % slots, :, : widths[q]], sems.at[i % slots]) for i, q in enumerate(places)
    ]
    for copy in copies[: slots - 1]:
        copy.start()
    for i, (q, copy) in enumerate(zip(places, copies)):
        if i + slots - 1 < len(copies):
            copies[i + slots - 1].start()
        copy.wait()
        outs[i][...] = dot(x[...], wide[i % slots, :, : widths[q]]).astype(BF16)


def base_chunks(places, widths, x, weight, token):
    feat, _ = weight.shape
    columns = sum(widths[q] for q in places)
    return pl.pallas_call(
        functools.partial(base_kernel, places, widths),
        out_shape=[jax.ShapeDtypeStruct((LIVE_ROWS, widths[q]), BF16) for q in places]
        + [jax.ShapeDtypeStruct(token.shape, token.dtype)],
        in_specs=[VMEM, ANY, ANY],
        out_specs=[VMEM] * len(places) + [ANY],
        input_output_aliases={2: len(places)},
        scratch_shapes=[pltpu.VMEM((3, feat, max(widths)), BF16), pltpu.SemaphoreType.DMA((3,))],
        compiler_params=params(),
        cost_estimate=cost(BASE_WORK * columns, columns),
        name="base",
    )(x, weight, token)


def odd_hop_kernel(base, got, token_in, out, token):
    out[...] = (base[...].astype(F32) + got[...].astype(F32)).astype(BF16)


def even_hop_kernel(near, far, got, token_in, out, token):
    @pl.when(is_inner())
    def _():
        out[...] = (near[...].astype(F32) + got[...].astype(F32)).astype(BF16)

    @pl.when(jnp.logical_not(is_inner()))
    def _():
        out[...] = far[...]


def hop(kernel, inputs, token, work=HOP_WORK):
    return pl.pallas_call(
        kernel,
        out_shape=(
            jax.ShapeDtypeStruct(inputs[0].shape, BF16),
            jax.ShapeDtypeStruct(token.shape, token.dtype),
        ),
        in_specs=[VMEM] * len(inputs) + [ANY],
        out_specs=(VMEM, ANY),
        input_output_aliases={len(inputs): 1},
        compiler_params=params(),
        cost_estimate=cost(work * inputs[0].size, 3 * inputs[0].size),
        name="hop",
    )(*inputs, token)


def fold(rank, adapters, half):
    shape = (adapters * rank, 2 * rank)
    return (iota(shape, 0) % rank + half * rank == iota(shape, 1)).astype(BF16)


def slot_mask(tag, rank, adapters):
    shape = (tag.shape[0], adapters * rank)
    return (iota(shape, 1) // rank).astype(F32) == tag.astype(F32)


def low_kernel(rank, blocks, down, *refs):
    parts, low = refs[:blocks], refs[blocks + 1]
    adapters = down.shape[0] // rank
    feat = down.shape[1]
    rows = parts[0].shape[0]
    half = blocks // 2
    maps = down[...]
    folds = [fold(rank, adapters, h) for h in range(2)]
    for k in range(half):
        total = None
        for h in range(2):
            part = parts[h * half + k]
            wide = dot_cols(part[:, :feat], maps)
            kept = jnp.where(slot_mask(part[:, feat : feat + 1], rank, adapters), wide, 0.0)
            got = dot(kept.astype(BF16), folds[h])
            total = got if total is None else total + got
        low[k * rows : (k + 1) * rows, :] = total.astype(BF16)


def low_values(parts, down, rank, token):
    rows, width = parts[0].shape
    blocks = len(parts)
    return pl.pallas_call(
        functools.partial(low_kernel, rank, blocks),
        out_shape=(
            jax.ShapeDtypeStruct((blocks // 2 * rows, 2 * rank), BF16),
            jax.ShapeDtypeStruct(token.shape, token.dtype),
        ),
        in_specs=[VMEM] * (blocks + 1) + [ANY],
        out_specs=(VMEM, ANY),
        input_output_aliases={blocks + 1: 1},
        compiler_params=params(),
        name="low",
    )(down, *parts, token)


def delta_kernel(rank, blocks, sums, up, *refs):
    tags, lows, outs = refs[:blocks], refs[blocks : blocks + sums], refs[blocks + sums + 1 :]
    adapters = up.shape[0] // rank
    rows = tags[0].shape[0]
    half = blocks // 2
    total = lows[0][...].astype(F32)
    for other in lows[1:]:
        total = total + other[...].astype(F32)
    low = total.astype(BF16)
    maps = up[...]
    for h in range(2):
        spread = fold(rank, adapters, h)
        for k in range(half):
            wide = dot_cols(low[k * rows : (k + 1) * rows, :], spread)
            mask = slot_mask(tags[h * half + k][:, :1], rank, adapters)
            kept = jnp.where(mask, wide, 0.0).astype(BF16)
            outs[h * half + k][...] = dot(kept, maps).astype(BF16)


def delta_values(parts, lows, up, rank, token):
    rows, width = parts[0].shape
    blocks = len(parts)
    columns = up.shape[1]
    tag = pl.BlockSpec((rows, TAG), lambda i: (0, width // TAG - 1))
    whole = lambda a: pl.BlockSpec(a.shape, lambda i: (0, 0))
    return pl.pallas_call(
        functools.partial(delta_kernel, rank, blocks, len(lows)),
        out_shape=[jax.ShapeDtypeStruct((rows, columns), BF16)] * blocks
        + [jax.ShapeDtypeStruct(token.shape, token.dtype)],
        grid=(1,),
        in_specs=[whole(up)] + [tag] * blocks + [whole(a) for a in lows] + [ANY],
        out_specs=[pl.BlockSpec((rows, columns), lambda i: (0, 0))] * blocks + [ANY],
        input_output_aliases={1 + blocks + len(lows): blocks},
        compiler_params=params(),
        name="delta",
    )(up, *parts, *lows, token)


def add_delta_kernel(per, place, *refs):
    bases, refs = refs[: 2 * per], refs[2 * per :]
    outs, parts = refs[-2 * per - 1 : -1], refs[: -2 * per - 2]
    rows = parts[0].shape[0]
    inner = is_inner()
    widths = tuple(base.shape[1] for base in bases[:per])
    for j in range(per):
        column = column_at(j, widths)
        total = None
        for k, part in enumerate(parts):
            got = dot(place[:, k * rows : (k + 1) * rows], part[:, pl.ds(column, widths[j])])
            total = got if total is None else total + got
        for i, mine in ((j, inner), (per + j, jnp.logical_not(inner))):
            wide = bases[i][...].astype(F32)
            outs[i][...] = (wide + jnp.where(mine, total, 0.0)).astype(BF16)


def add_delta(bases, place, parts, token):
    per = len(bases) // 2
    inputs = [place, *bases, *parts]
    return pl.pallas_call(
        functools.partial(add_delta_kernel, per),
        out_shape=[jax.ShapeDtypeStruct(base.shape, BF16) for base in bases]
        + [jax.ShapeDtypeStruct(token.shape, token.dtype)],
        in_specs=[VMEM] * len(inputs) + [ANY],
        out_specs=[VMEM] * len(bases) + [ANY],
        input_output_aliases={len(inputs): len(bases)},
        compiler_params=params(),
        name="add_delta",
    )(*inputs, token)


def finish_kernel(widths, near_q, far_q, *refs):
    refs = list(refs)
    near = refs.pop(0) if near_q is not None else None
    far = refs.pop(0) if far_q is not None else None
    even, odd = refs.pop(0), refs.pop(0) if near_q is not None else None
    pick = refs.pop(0)
    out, _, made, sems = refs[-4:]

    def write(q, terms):
        column, width = column_at(q, widths), widths[q]
        cut = width // LANES // 2 * LANES
        copies = []
        for i, here in enumerate((slice(0, cut), slice(cut, width))):
            total = sum(term[:, here].astype(F32) for term in terms)
            made[:, here] = dot(pick[...], total.astype(BF16)).astype(BF16)
            there = pl.ds(pl.multiple_of(column + here.start, LANES), here.stop - here.start)
            copies.append(pltpu.make_async_copy(made.at[:, here], out.at[:, there], sems.at[i]))
            copies[-1].start()
        for copy in copies:
            copy.wait()

    if near_q is not None:

        @pl.when(is_inner())
        def _():
            write(near_q, [near, even, odd])

    if far_q is not None:

        @pl.when(jnp.logical_not(is_inner()))
        def _():
            write(far_q, [far, even])


def finish(near_q, far_q, widths, bases, even, odd, pick, held, token):
    rows, width = pick.shape[0], even.shape[1]
    inputs = [bases[q] for q in (near_q, far_q) if q is not None] + [even]
    inputs += [odd] if near_q is not None else []
    inputs += [pick]
    last = [token] if held is None else [held, token]
    aliases = {len(inputs) + len(last) - 1: 1}
    if held is not None:
        aliases[len(inputs)] = 0
    return pl.pallas_call(
        functools.partial(finish_kernel, widths, near_q, far_q),
        out_shape=(
            jax.ShapeDtypeStruct((rows, sum(widths)), BF16),
            jax.ShapeDtypeStruct(token.shape, token.dtype),
        ),
        in_specs=[VMEM] * len(inputs) + [ANY] * len(last),
        out_specs=(ANY, ANY),
        scratch_shapes=[pltpu.VMEM((rows, width), BF16), pltpu.SemaphoreType.DMA((2,))],
        input_output_aliases=aliases,
        compiler_params=params(),
        cost_estimate=cost(2 * LIVE_ROWS * rows * width, 6 * LIVE_ROWS * width),
        name="finish",
    )(*inputs, *last)


def send_groups(blocks):
    replicas = lax.axis_size("replica")
    parts = [blocks[0]]
    for k in range(1, replicas):
        hops = [(i, (i + k) % replicas) for i in range(replicas)]
        parts.append(lax.ppermute(blocks[k], "replica", hops))
    return parts


def send_lows(low):
    shards = lax.axis_size("tensor")
    if shards > 4:
        return [lax.psum(low, "tensor")]
    lows = [low]
    for k in range(1, shards):
        hops = [(i, (i + k) % shards) for i in range(shards)]
        lows.append(lax.ppermute(low, "tensor", hops))
    return lows


def send_back(made):
    replicas = lax.axis_size("replica")
    back = [made[0]]
    for k in range(1, replicas):
        hops = [(i, (i - k) % replicas) for i in range(replicas)]
        back.append(lax.ppermute(made[k], "replica", hops))
    return back


def on_device(x, owner, slot, live, weight, down, up):
    width = weight.shape[1]
    rank = down.shape[1]
    replicas, shards = lax.axis_size("replica"), lax.axis_size("tensor")
    down, up = down.reshape(-1, down.shape[2]), up.reshape(-1, up.shape[2])
    token = jnp.zeros((8, 128), jnp.int32)
    if shards != 4:
        compact_x, pick, place, spread, tags = prepare(owner[:, 0], slot, live[0], x, replicas)
        *blocks, token = spread_groups(spread, tags, x, token)
        z, share = lax.axis_index("tensor").astype(jnp.int32), width // shards
        base = dot(compact_x, weight)
        parts = send_groups(blocks)
        low, token = low_values(parts, down, rank, token)
        *made, token = delta_values(parts, send_lows(low), up, rank, token)
        back = jnp.concatenate(send_back(made), axis=0)
        mine = lax.dynamic_slice_in_dim(base, z * share, share, 1) + dot(place, back)
        base = lax.dynamic_update_slice_in_dim(base, mine, z * share, 1).astype(BF16)
        total = lax.psum_scatter(base, "tensor", scatter_dimension=1, tiled=True)
        total = lax.all_gather(total, "tensor", axis=1, tiled=True)
        return dot(pick, total).astype(BF16)

    widths = widths_of(width, shards)
    chunks, per = len(widths), len(widths) // shards
    even = [(0, 1), (1, 0), (2, 3), (3, 2)]
    odd = [(1, 2), (2, 1)]
    opened = prepare(owner[:, 0], slot, live[0], x, replicas, weight, widths)
    compact_x, pick, place, spread, tags, message = opened
    evens, odds = {0: lax.ppermute(message, "tensor", even)}, {}
    *blocks, token = spread_groups(spread, tags, x, token)
    parts = send_groups(blocks)
    *early, token = base_chunks((1, 2), widths, compact_x, weight, token)
    bases = [message, *early]
    for step in (1, 2):
        evens[step] = lax.ppermute(bases[step], "tensor", even)
    *late, token = base_chunks(tuple(range(3, chunks)), widths, compact_x, weight, token)
    bases += late
    low, token = low_values(parts, down, rank, token)
    lows = send_lows(low)
    steps = chunks + 3
    result = None
    unfinished = list(range(steps))
    seen_even, seen_odd = set(), set()

    def close(result, token):
        for a in list(unfinished):
            b = chunks - a
            if a not in seen_even or (1 <= b <= chunks and b not in seen_odd):
                continue
            unfinished.remove(a)
            near_q = chunks - 1 - a if a < chunks else None
            far_q = chunks + 2 - a if a >= 3 else None
            result, token = finish(near_q, far_q, widths, bases, evens[a], odds.get(b), pick, result, token)
        return result, token

    for step in range(1, steps):
        if step >= 3:
            far = bases[step] if step < chunks else bases[step - 3]
            inputs = [bases[step - 3], far, odds[step - 2]]
            message, token = hop(even_hop_kernel, inputs, token)
            evens[step] = lax.ppermute(message, "tensor", even)
            seen_odd.add(step - 2)
            result, token = close(result, token)
        if step <= chunks:
            work = FIRST_HOP_WORK if step == 1 else HOP_WORK
            message, token = hop(odd_hop_kernel, [bases[chunks - step], evens[step - 1]], token, work)
            odds[step] = lax.ppermute(message, "tensor", odd)
        seen_even.add(step - 1)
        if step == DELTA_AT:
            *made, token = delta_values(parts, lows, up, rank, token)
            back = send_back(made)
        if step == per + 2:
            own = list(range(per, 2 * per)) + list(range(3 * per, 4 * per))
            *summed, token = add_delta([bases[q] for q in own], place, back, token)
            for q, value in zip(own, summed):
                bases[q] = value
        result, token = close(result, token)
    seen_even.add(steps - 1)
    result, token = close(result, token)
    return result


def solution(mesh):
    placed = (
        P(("parts", "replica"), "tensor"),
        P(("parts", "replica"), None),
        P(("parts", "replica")),
        P(("parts", "replica"), None),
        P("tensor", None),
        P("replica", None, "tensor"),
        P("replica", None, "tensor"),
    )
    return jax.shard_map(
        on_device,
        mesh=mesh,
        in_specs=placed,
        out_specs=P(("parts", "replica"), None),
        check_vma=False,
    )
```

```python
import functools

import jax
import jax.numpy as jnp
from jax import lax
from jax.experimental import pallas as pl
from jax.experimental.pallas import tpu as pltpu
from jax.sharding import PartitionSpec as P

GROUP_ROWS = 16
CAP = 4
LIVE_ROWS = 224
TAG = 128
LANES = 128
CUTS = 3
BF16 = jnp.bfloat16
F32 = jnp.float32
MIB = 1024 * 1024
HOP_WORK = 14000
FIRST_HOP_WORK = 8000
BASE_WORK = 400000
PREPARE_MIB = 60
DELTA_AT = 3


def dot(a, b):
    return jnp.dot(a, b, preferred_element_type=F32)


def dot_cols(a, b):
    return lax.dot_general(a, b, (((1,), (1,)), ((), ())), preferred_element_type=F32)


def iota(shape, dim):
    return lax.broadcasted_iota(jnp.int32, shape, dim)


def params(mib=50):
    return pltpu.CompilerParams(vmem_limit_bytes=mib * MIB)


def cost(flops, elements):
    return pl.CostEstimate(flops=flops, bytes_accessed=2 * elements, transcendentals=0)


ANY = pl.BlockSpec(memory_space=pl.ANY)
VMEM = pl.BlockSpec(memory_space=pltpu.VMEM)


def is_inner():
    z = lax.axis_index("tensor")
    return (z == 1) | (z == 2)


def widths_of(width, shards):
    tiles = width // shards // LANES
    if CUTS == 3:
        side = tiles // 3
        cuts = (side, tiles - 2 * side, side)
    else:
        cuts = (tiles // CUTS,) * CUTS
    return tuple(cut * LANES for cut in cuts) * shards


def column_at(q, widths):
    left, right = sum(widths[:q]), sum(widths[: len(widths) - 1 - q])
    column = jnp.where(lax.axis_index("tensor") % 2 == 0, right, left)
    return pl.multiple_of(column, LANES)


def weight_copy(w, q, widths, into, sem):
    return pltpu.make_async_copy(w.at[:, pl.ds(column_at(q, widths), widths[q])], into, sem)


def prepare_kernel(replicas, widths, owner_in, slot_in, live_in, x_in, *refs):
    refs = list(refs)
    line = widths is not None
    w = refs.pop(0) if line else None
    compact_x, pick, place, spread_out, tags_out = refs[:5]
    message = refs[5] if line else None
    owner, slot, live, x, sems = refs[-5:]
    wide, wide_sem = (refs[-7], refs[-6]) if line else (None, None)
    copies = [
        pltpu.make_async_copy(src, dst, sems.at[i])
        for i, (src, dst) in enumerate(((owner_in, owner), (slot_in, slot), (live_in, live), (x_in, x)))
    ]
    for copy in copies:
        copy.start()
    if line:
        weights = weight_copy(w, 0, widths, wide, wide_sem.at[0])
        weights.start()
    for copy in copies:
        copy.wait()
    me = lax.axis_index("replica")
    rows, feat = x.shape
    groups = rows // GROUP_ROWS
    out_rows = replicas * CAP * GROUP_ROWS
    lane = iota((1, rows), 1)
    lane_group, lane_slot = lane // GROUP_ROWS, lane % GROUP_ROWS
    row_group = iota((rows, TAG), 0) // GROUP_ROWS
    packed = jnp.full((1, rows), -1, jnp.int32)
    target = jnp.zeros((1, rows), jnp.int32)
    tags = jnp.zeros((rows, TAG), F32)
    owners = [owner[g] for g in range(groups)]
    offset = jnp.int32(0)
    used = [jnp.int32(0)] * replicas
    for g in range(groups):
        count = live[g]
        mine = lane_group == g
        packed = jnp.where(mine & (lane_slot < count), offset + lane_slot, packed)
        offset = offset + count
        position = jnp.int32(0)
        for o in range(replicas):
            hit = owners[g] == o
            position = jnp.where(hit, used[o], position)
            used[o] = used[o] + hit.astype(jnp.int32)
        hop = lax.rem(owners[g] - me + replicas, replicas)
        start = (hop * CAP + position) * GROUP_ROWS
        target = jnp.where(mine, start + lane_slot, target)
        tags = jnp.where(row_group == g, slot[g].astype(F32), tags)
    compact = (iota((LIVE_ROWS, rows), 0) == packed).astype(BF16)
    spread = (iota((out_rows, rows), 0) == target).astype(BF16)
    pick[...] = compact.astype(F32).T.astype(BF16)
    place[...] = dot_cols(compact, spread).astype(BF16)
    packed_x = dot(compact, x[...]).astype(BF16)
    compact_x[...] = packed_x
    spread_out[...] = spread
    tags_out[...] = tags.astype(BF16)
    if line:
        weights.wait()
        message[...] = dot(packed_x, wide[...]).astype(BF16)


def prepare(owner, slot, live, x, replicas, weight=None, widths=None):
    rows, feat = x.shape
    block = CAP * GROUP_ROWS
    line = weight is not None
    shape = lambda *dims: jax.ShapeDtypeStruct(dims, BF16)
    outs = [shape(LIVE_ROWS, feat), shape(rows, LIVE_ROWS), shape(LIVE_ROWS, replicas * block)]
    outs += [shape(replicas * block, rows), shape(rows, TAG)]
    scratch = [pltpu.SMEM(a.shape, jnp.int32) for a in (owner, slot, live)]
    scratch += [pltpu.VMEM(x.shape, BF16), pltpu.SemaphoreType.DMA((4,))]
    if line:
        outs.append(shape(LIVE_ROWS, widths[0]))
        scratch = [pltpu.VMEM((feat, widths[0]), BF16), pltpu.SemaphoreType.DMA((1,))] + scratch
    return pl.pallas_call(
        functools.partial(prepare_kernel, replicas, widths),
        out_shape=outs,
        in_specs=[ANY] * (5 if line else 4),
        out_specs=[VMEM] * len(outs),
        scratch_shapes=scratch,
        compiler_params=params(PREPARE_MIB),
        name="prepare",
    )(owner, slot, live, x, *([weight] if line else []))


def spread_kernel(spread, tags, x, token_in, *blocks):
    feat = x.shape[1]
    sent = dot(spread[...], x[...]).astype(BF16)
    sent_tags = dot(spread[...], tags[...]).astype(BF16)
    for k, block in enumerate(blocks[:-1]):
        here = slice(k * block.shape[0], (k + 1) * block.shape[0])
        block[:, :feat] = sent[here]
        block[:, feat:] = sent_tags[here]


def spread_groups(spread, tags, x, token):
    rows = CAP * GROUP_ROWS
    blocks = spread.shape[0] // rows
    return pl.pallas_call(
        spread_kernel,
        out_shape=[jax.ShapeDtypeStruct((rows, x.shape[1] + TAG), BF16)] * blocks
        + [jax.ShapeDtypeStruct(token.shape, token.dtype)],
        in_specs=[VMEM] * 3 + [ANY],
        out_specs=[VMEM] * blocks + [ANY],
        input_output_aliases={3: blocks},
        compiler_params=params(),
        name="spread",
    )(spread, tags, x, token)


def base_kernel(places, widths, x, w, token_in, *refs):
    outs, wide, sems = refs[: len(places)], refs[-2], refs[-1]
    slots = wide.shape[0]
    copies = [
        weight_copy(w, q, widths, wide.at[i % slots, :, : widths[q]], sems.at[i % slots]) for i, q in enumerate(places)
    ]
    for copy in copies[: slots - 1]:
        copy.start()
    for i, (q, copy) in enumerate(zip(places, copies)):
        if i + slots - 1 < len(copies):
            copies[i + slots - 1].start()
        copy.wait()
        outs[i][...] = dot(x[...], wide[i % slots, :, : widths[q]]).astype(BF16)


def base_chunks(places, widths, x, weight, token):
    feat, _ = weight.shape
    columns = sum(widths[q] for q in places)
    return pl.pallas_call(
        functools.partial(base_kernel, places, widths),
        out_shape=[jax.ShapeDtypeStruct((LIVE_ROWS, widths[q]), BF16) for q in places]
        + [jax.ShapeDtypeStruct(token.shape, token.dtype)],
        in_specs=[VMEM, ANY, ANY],
        out_specs=[VMEM] * len(places) + [ANY],
        input_output_aliases={2: len(places)},
        scratch_shapes=[pltpu.VMEM((3, feat, max(widths)), BF16), pltpu.SemaphoreType.DMA((3,))],
        compiler_params=params(),
        cost_estimate=cost(BASE_WORK * columns, columns),
        name="base",
    )(x, weight, token)


def odd_hop_kernel(base, got, token_in, out, token):
    out[...] = (base[...].astype(F32) + got[...].astype(F32)).astype(BF16)


def even_hop_kernel(near, far, got, token_in, out, token):
    @pl.when(is_inner())
    def _():
        out[...] = (near[...].astype(F32) + got[...].astype(F32)).astype(BF16)

    @pl.when(jnp.logical_not(is_inner()))
    def _():
        out[...] = far[...]


def hop(kernel, inputs, token, work=HOP_WORK):
    return pl.pallas_call(
        kernel,
        out_shape=(
            jax.ShapeDtypeStruct(inputs[0].shape, BF16),
            jax.ShapeDtypeStruct(token.shape, token.dtype),
        ),
        in_specs=[VMEM] * len(inputs) + [ANY],
        out_specs=(VMEM, ANY),
        input_output_aliases={len(inputs): 1},
        compiler_params=params(),
        cost_estimate=cost(work * inputs[0].size, 3 * inputs[0].size),
        name="hop",
    )(*inputs, token)


def fold(rank, adapters, half):
    shape = (adapters * rank, 2 * rank)
    return (iota(shape, 0) % rank + half * rank == iota(shape, 1)).astype(BF16)


def slot_mask(tag, rank, adapters):
    shape = (tag.shape[0], adapters * rank)
    return (iota(shape, 1) // rank).astype(F32) == tag.astype(F32)


def low_kernel(rank, blocks, down, *refs):
    parts, low = refs[:blocks], refs[blocks + 1]
    adapters = down.shape[0] // rank
    feat = down.shape[1]
    rows = parts[0].shape[0]
    half = blocks // 2
    maps = down[...]
    folds = [fold(rank, adapters, h) for h in range(2)]
    for k in range(half):
        total = None
        for h in range(2):
            part = parts[h * half + k]
            wide = dot_cols(part[:, :feat], maps)
            kept = jnp.where(slot_mask(part[:, feat : feat + 1], rank, adapters), wide, 0.0)
            got = dot(kept.astype(BF16), folds[h])
            total = got if total is None else total + got
        low[k * rows : (k + 1) * rows, :] = total.astype(BF16)


def low_values(parts, down, rank, token):
    rows, width = parts[0].shape
    blocks = len(parts)
    return pl.pallas_call(
        functools.partial(low_kernel, rank, blocks),
        out_shape=(
            jax.ShapeDtypeStruct((blocks // 2 * rows, 2 * rank), BF16),
            jax.ShapeDtypeStruct(token.shape, token.dtype),
        ),
        in_specs=[VMEM] * (blocks + 1) + [ANY],
        out_specs=(VMEM, ANY),
        input_output_aliases={blocks + 1: 1},
        compiler_params=params(),
        name="low",
    )(down, *parts, token)


def delta_kernel(rank, blocks, sums, up, *refs):
    tags, lows, outs = refs[:blocks], refs[blocks : blocks + sums], refs[blocks + sums + 1 :]
    adapters = up.shape[0] // rank
    rows = tags[0].shape[0]
    half = blocks // 2
    total = lows[0][...].astype(F32)
    for other in lows[1:]:
        total = total + other[...].astype(F32)
    low = total.astype(BF16)
    maps = up[...]
    for h in range(2):
        spread = fold(rank, adapters, h)
        for k in range(half):
            wide = dot_cols(low[k * rows : (k + 1) * rows, :], spread)
            mask = slot_mask(tags[h * half + k][:, :1], rank, adapters)
            kept = jnp.where(mask, wide, 0.0).astype(BF16)
            outs[h * half + k][...] = dot(kept, maps).astype(BF16)


def delta_values(parts, lows, up, rank, token):
    rows, width = parts[0].shape
    blocks = len(parts)
    columns = up.shape[1]
    tag = pl.BlockSpec((rows, TAG), lambda i: (0, width // TAG - 1))
    whole = lambda a: pl.BlockSpec(a.shape, lambda i: (0, 0))
    return pl.pallas_call(
        functools.partial(delta_kernel, rank, blocks, len(lows)),
        out_shape=[jax.ShapeDtypeStruct((rows, columns), BF16)] * blocks
        + [jax.ShapeDtypeStruct(token.shape, token.dtype)],
        grid=(1,),
        in_specs=[whole(up)] + [tag] * blocks + [whole(a) for a in lows] + [ANY],
        out_specs=[pl.BlockSpec((rows, columns), lambda i: (0, 0))] * blocks + [ANY],
        input_output_aliases={1 + blocks + len(lows): blocks},
        compiler_params=params(),
        name="delta",
    )(up, *parts, *lows, token)


def add_delta_kernel(per, place, *refs):
    bases, refs = refs[: 2 * per], refs[2 * per :]
    outs, parts = refs[-2 * per - 1 : -1], refs[: -2 * per - 2]
    rows = parts[0].shape[0]
    inner = is_inner()
    widths = tuple(base.shape[1] for base in bases[:per])
    for j in range(per):
        column = column_at(j, widths)
        total = None
        for k, part in enumerate(parts):
            got = dot(place[:, k * rows : (k + 1) * rows], part[:, pl.ds(column, widths[j])])
            total = got if total is None else total + got
        for i, mine in ((j, inner), (per + j, jnp.logical_not(inner))):
            wide = bases[i][...].astype(F32)
            outs[i][...] = (wide + jnp.where(mine, total, 0.0)).astype(BF16)


def add_delta(bases, place, parts, token):
    per = len(bases) // 2
    inputs = [place, *bases, *parts]
    return pl.pallas_call(
        functools.partial(add_delta_kernel, per),
        out_shape=[jax.ShapeDtypeStruct(base.shape, BF16) for base in bases]
        + [jax.ShapeDtypeStruct(token.shape, token.dtype)],
        in_specs=[VMEM] * len(inputs) + [ANY],
        out_specs=[VMEM] * len(bases) + [ANY],
        input_output_aliases={len(inputs): len(bases)},
        compiler_params=params(),
        name="add_delta",
    )(*inputs, token)


def finish_kernel(widths, near_q, far_q, *refs):
    refs = list(refs)
    near = refs.pop(0) if near_q is not None else None
    far = refs.pop(0) if far_q is not None else None
    even, odd = refs.pop(0), refs.pop(0) if near_q is not None else None
    pick = refs.pop(0)
    out, _, made, sems = refs[-4:]

    def write(q, terms):
        column, width = column_at(q, widths), widths[q]
        cut = width // LANES // 2 * LANES
        copies = []
        for i, here in enumerate((slice(0, cut), slice(cut, width))):
            total = sum(term[:, here].astype(F32) for term in terms)
            made[:, here] = dot(pick[...], total.astype(BF16)).astype(BF16)
            there = pl.ds(pl.multiple_of(column + here.start, LANES), here.stop - here.start)
            copies.append(pltpu.make_async_copy(made.at[:, here], out.at[:, there], sems.at[i]))
            copies[-1].start()
        for copy in copies:
            copy.wait()

    if near_q is not None:

        @pl.when(is_inner())
        def _():
            write(near_q, [near, even, odd])

    if far_q is not None:

        @pl.when(jnp.logical_not(is_inner()))
        def _():
            write(far_q, [far, even])


def finish(near_q, far_q, widths, bases, even, odd, pick, held, token):
    rows, width = pick.shape[0], even.shape[1]
    inputs = [bases[q] for q in (near_q, far_q) if q is not None] + [even]
    inputs += [odd] if near_q is not None else []
    inputs += [pick]
    last = [token] if held is None else [held, token]
    aliases = {len(inputs) + len(last) - 1: 1}
    if held is not None:
        aliases[len(inputs)] = 0
    return pl.pallas_call(
        functools.partial(finish_kernel, widths, near_q, far_q),
        out_shape=(
            jax.ShapeDtypeStruct((rows, sum(widths)), BF16),
            jax.ShapeDtypeStruct(token.shape, token.dtype),
        ),
        in_specs=[VMEM] * len(inputs) + [ANY] * len(last),
        out_specs=(ANY, ANY),
        scratch_shapes=[pltpu.VMEM((rows, width), BF16), pltpu.SemaphoreType.DMA((2,))],
        input_output_aliases=aliases,
        compiler_params=params(),
        cost_estimate=cost(2 * LIVE_ROWS * rows * width, 6 * LIVE_ROWS * width),
        name="finish",
    )(*inputs, *last)


def send_groups(blocks):
    replicas = lax.axis_size("replica")
    parts = [blocks[0]]
    for k in range(1, replicas):
        hops = [(i, (i + k) % replicas) for i in range(replicas)]
        parts.append(lax.ppermute(blocks[k], "replica", hops))
    return parts


def send_lows(low):
    shards = lax.axis_size("tensor")
    if shards > 4:
        return [lax.psum(low, "tensor")]
    lows = [low]
    for k in range(1, shards):
        hops = [(i, (i + k) % shards) for i in range(shards)]
        lows.append(lax.ppermute(low, "tensor", hops))
    return lows


def send_back(made):
    replicas = lax.axis_size("replica")
    back = [made[0]]
    for k in range(1, replicas):
        hops = [(i, (i - k) % replicas) for i in range(replicas)]
        back.append(lax.ppermute(made[k], "replica", hops))
    return back


def on_device(x, owner, slot, live, weight, down, up):
    width = weight.shape[1]
    rank = down.shape[1]
    replicas, shards = lax.axis_size("replica"), lax.axis_size("tensor")
    down, up = down.reshape(-1, down.shape[2]), up.reshape(-1, up.shape[2])
    token = jnp.zeros((8, 128), jnp.int32)
    if shards != 4:
        compact_x, pick, place, spread, tags = prepare(owner[:, 0], slot, live[0], x, replicas)
        *blocks, token = spread_groups(spread, tags, x, token)
        z, share = lax.axis_index("tensor").astype(jnp.int32), width // shards
        base = dot(compact_x, weight)
        parts = send_groups(blocks)
        low, token = low_values(parts, down, rank, token)
        *made, token = delta_values(parts, send_lows(low), up, rank, token)
        back = jnp.concatenate(send_back(made), axis=0)
        mine = lax.dynamic_slice_in_dim(base, z * share, share, 1) + dot(place, back)
        base = lax.dynamic_update_slice_in_dim(base, mine, z * share, 1).astype(BF16)
        total = lax.psum_scatter(base, "tensor", scatter_dimension=1, tiled=True)
        total = lax.all_gather(total, "tensor", axis=1, tiled=True)
        return dot(pick, total).astype(BF16)

    widths = widths_of(width, shards)
    chunks, per = len(widths), len(widths) // shards
    even = [(0, 1), (1, 0), (2, 3), (3, 2)]
    odd = [(1, 2), (2, 1)]
    opened = prepare(owner[:, 0], slot, live[0], x, replicas, weight, widths)
    compact_x, pick, place, spread, tags, message = opened
    evens, odds = {0: lax.ppermute(message, "tensor", even)}, {}
    *blocks, token = spread_groups(spread, tags, x, token)
    parts = send_groups(blocks)
    *early, token = base_chunks((1, 2), widths, compact_x, weight, token)
    bases = [message, *early]
    for step in (1, 2):
        evens[step] = lax.ppermute(bases[step], "tensor", even)
    *late, token = base_chunks(tuple(range(3, chunks)), widths, compact_x, weight, token)
    bases += late
    low, token = low_values(parts, down, rank, token)
    lows = send_lows(low)
    steps = chunks + 3
    result = None
    unfinished = list(range(steps))
    seen_even, seen_odd = set(), set()

    def close(result, token):
        for a in list(unfinished):
            b = chunks - a
            if a not in seen_even or (1 <= b <= chunks and b not in seen_odd):
                continue
            unfinished.remove(a)
            near_q = chunks - 1 - a if a < chunks else None
            far_q = chunks + 2 - a if a >= 3 else None
            result, token = finish(near_q, far_q, widths, bases, evens[a], odds.get(b), pick, result, token)
        return result, token

    for step in range(1, steps):
        if step >= 3:
            far = bases[step] if step < chunks else bases[step - 3]
            inputs = [bases[step - 3], far, odds[step - 2]]
            message, token = hop(even_hop_kernel, inputs, token)
            evens[step] = lax.ppermute(message, "tensor", even)
            seen_odd.add(step - 2)
            result, token = close(result, token)
        if step <= chunks:
            work = FIRST_HOP_WORK if step == 1 else HOP_WORK
            message, token = hop(odd_hop_kernel, [bases[chunks - step], evens[step - 1]], token, work)
            odds[step] = lax.ppermute(message, "tensor", odd)
        seen_even.add(step - 1)
        if step == DELTA_AT:
            *made, token = delta_values(parts, lows, up, rank, token)
            back = send_back(made)
        if step == per + 2:
            own = list(range(per, 2 * per)) + list(range(3 * per, 4 * per))
            *summed, token = add_delta([bases[q] for q in own], place, back, token)
            for q, value in zip(own, summed):
                bases[q] = value
        result, token = close(result, token)
    seen_even.add(steps - 1)
    result, token = close(result, token)
    return result


def solution(mesh):
    placed = (
        P(("parts", "replica"), "tensor"),
        P(("parts", "replica"), None),
        P(("parts", "replica")),
        P(("parts", "replica"), None),
        P("tensor", None),
        P("replica", None, "tensor"),
        P("replica", None, "tensor"),
    )
    return jax.shard_map(
        on_device,
        mesh=mesh,
        in_specs=placed,
        out_specs=P(("parts", "replica"), None),
        check_vma=False,
    )
```

```python
import functools

import jax
import jax.numpy as jnp
from jax import lax
from jax.experimental import pallas as pl
from jax.experimental.pallas import tpu as pltpu
from jax.sharding import PartitionSpec as P

GROUP_ROWS = 16
CAP = 4
LIVE_ROWS = 224
TAG = 128
LANES = 128
CUTS = 3
BF16 = jnp.bfloat16
F32 = jnp.float32
MIB = 1024 * 1024
HOP_WORK = 8000
FIRST_HOP_WORK = 8000
BASE_WORK = 400000
PREPARE_MIB = 60
DELTA_AT = 3


def dot(a, b):
    return jnp.dot(a, b, preferred_element_type=F32)


def dot_cols(a, b):
    return lax.dot_general(a, b, (((1,), (1,)), ((), ())), preferred_element_type=F32)


def iota(shape, dim):
    return lax.broadcasted_iota(jnp.int32, shape, dim)


def params(mib=50):
    return pltpu.CompilerParams(vmem_limit_bytes=mib * MIB)


def cost(flops, elements):
    return pl.CostEstimate(flops=flops, bytes_accessed=2 * elements, transcendentals=0)


ANY = pl.BlockSpec(memory_space=pl.ANY)
VMEM = pl.BlockSpec(memory_space=pltpu.VMEM)


def is_inner():
    z = lax.axis_index("tensor")
    return (z == 1) | (z == 2)


def widths_of(width, shards):
    tiles = width // shards // LANES
    if CUTS == 3:
        side = tiles // 3
        cuts = (side, tiles - 2 * side, side)
    else:
        cuts = (tiles // CUTS,) * CUTS
    return tuple(cut * LANES for cut in cuts) * shards


def column_at(q, widths):
    left, right = sum(widths[:q]), sum(widths[: len(widths) - 1 - q])
    column = jnp.where(lax.axis_index("tensor") % 2 == 0, right, left)
    return pl.multiple_of(column, LANES)


def weight_copy(w, q, widths, into, sem):
    return pltpu.make_async_copy(w.at[:, pl.ds(column_at(q, widths), widths[q])], into, sem)


def prepare_kernel(replicas, widths, owner_in, slot_in, live_in, x_in, *refs):
    refs = list(refs)
    line = widths is not None
    w = refs.pop(0) if line else None
    compact_x, pick, place = refs[:3]
    blocks = refs[3 : 3 + replicas]
    message = refs[3 + replicas] if line else None
    owner, slot, live, x, sems = refs[-5:]
    wide, wide_sem = (refs[-7], refs[-6]) if line else (None, None)
    copies = [
        pltpu.make_async_copy(src, dst, sems.at[i])
        for i, (src, dst) in enumerate(((owner_in, owner), (slot_in, slot), (live_in, live), (x_in, x)))
    ]
    for copy in copies:
        copy.start()
    if line:
        weights = weight_copy(w, 0, widths, wide, wide_sem.at[0])
        weights.start()
    for copy in copies:
        copy.wait()
    me = lax.axis_index("replica")
    rows, feat = x.shape
    groups = rows // GROUP_ROWS
    out_rows = replicas * CAP * GROUP_ROWS
    lane = iota((1, rows), 1)
    lane_group, lane_slot = lane // GROUP_ROWS, lane % GROUP_ROWS
    row_group = iota((rows, TAG), 0) // GROUP_ROWS
    packed = jnp.full((1, rows), -1, jnp.int32)
    target = jnp.zeros((1, rows), jnp.int32)
    tags = jnp.zeros((rows, TAG), F32)
    owners = [owner[g] for g in range(groups)]
    offset = jnp.int32(0)
    used = [jnp.int32(0)] * replicas
    for g in range(groups):
        count = live[g]
        mine = lane_group == g
        packed = jnp.where(mine & (lane_slot < count), offset + lane_slot, packed)
        offset = offset + count
        position = jnp.int32(0)
        for o in range(replicas):
            hit = owners[g] == o
            position = jnp.where(hit, used[o], position)
            used[o] = used[o] + hit.astype(jnp.int32)
        hop = lax.rem(owners[g] - me + replicas, replicas)
        start = (hop * CAP + position) * GROUP_ROWS
        target = jnp.where(mine, start + lane_slot, target)
        tags = jnp.where(row_group == g, slot[g].astype(F32), tags)
    compact = (iota((LIVE_ROWS, rows), 0) == packed).astype(BF16)
    spread = (iota((out_rows, rows), 0) == target).astype(BF16)
    pick[...] = compact.astype(F32).T.astype(BF16)
    place[...] = dot_cols(compact, spread).astype(BF16)
    packed_x = dot(compact, x[...]).astype(BF16)
    compact_x[...] = packed_x
    sent = dot(spread, x[...]).astype(BF16)
    sent_tags = dot(spread, tags.astype(BF16)).astype(BF16)
    for k, block in enumerate(blocks):
        here = slice(k * block.shape[0], (k + 1) * block.shape[0])
        block[:, :feat] = sent[here]
        block[:, feat:] = sent_tags[here]
    if line:
        weights.wait()
        message[...] = dot(packed_x, wide[...]).astype(BF16)


def prepare(owner, slot, live, x, replicas, weight=None, widths=None):
    rows, feat = x.shape
    block = CAP * GROUP_ROWS
    line = weight is not None
    shape = lambda *dims: jax.ShapeDtypeStruct(dims, BF16)
    outs = [shape(LIVE_ROWS, feat), shape(rows, LIVE_ROWS), shape(LIVE_ROWS, replicas * block)]
    outs += [shape(block, feat + TAG)] * replicas
    scratch = [pltpu.SMEM(a.shape, jnp.int32) for a in (owner, slot, live)]
    scratch += [pltpu.VMEM(x.shape, BF16), pltpu.SemaphoreType.DMA((4,))]
    if line:
        outs.append(shape(LIVE_ROWS, widths[0]))
        scratch = [pltpu.VMEM((feat, widths[0]), BF16), pltpu.SemaphoreType.DMA((1,))] + scratch
    return pl.pallas_call(
        functools.partial(prepare_kernel, replicas, widths),
        out_shape=outs,
        in_specs=[ANY] * (5 if line else 4),
        out_specs=[VMEM] * len(outs),
        scratch_shapes=scratch,
        compiler_params=params(PREPARE_MIB),
        name="prepare",
    )(owner, slot, live, x, *([weight] if line else []))


def base_kernel(places, widths, x, w, token_in, *refs):
    outs, wide, sems = refs[: len(places)], refs[-2], refs[-1]
    slots = wide.shape[0]
    copies = [
        weight_copy(w, q, widths, wide.at[i % slots, :, : widths[q]], sems.at[i % slots]) for i, q in enumerate(places)
    ]
    for copy in copies[: slots - 1]:
        copy.start()
    for i, (q, copy) in enumerate(zip(places, copies)):
        if i + slots - 1 < len(copies):
            copies[i + slots - 1].start()
        copy.wait()
        outs[i][...] = dot(x[...], wide[i % slots, :, : widths[q]]).astype(BF16)


def base_chunks(places, widths, x, weight, token):
    feat, _ = weight.shape
    columns = sum(widths[q] for q in places)
    return pl.pallas_call(
        functools.partial(base_kernel, places, widths),
        out_shape=[jax.ShapeDtypeStruct((LIVE_ROWS, widths[q]), BF16) for q in places]
        + [jax.ShapeDtypeStruct(token.shape, token.dtype)],
        in_specs=[VMEM, ANY, ANY],
        out_specs=[VMEM] * len(places) + [ANY],
        input_output_aliases={2: len(places)},
        scratch_shapes=[pltpu.VMEM((3, feat, max(widths)), BF16), pltpu.SemaphoreType.DMA((3,))],
        compiler_params=params(),
        cost_estimate=cost(BASE_WORK * columns, columns),
        name="base",
    )(x, weight, token)


def odd_hop_kernel(base, got, token_in, out, token):
    out[...] = (base[...].astype(F32) + got[...].astype(F32)).astype(BF16)


def even_hop_kernel(near, far, got, token_in, out, token):
    @pl.when(is_inner())
    def _():
        out[...] = (near[...].astype(F32) + got[...].astype(F32)).astype(BF16)

    @pl.when(jnp.logical_not(is_inner()))
    def _():
        out[...] = far[...]


def hop(kernel, inputs, token, work=HOP_WORK):
    return pl.pallas_call(
        kernel,
        out_shape=(
            jax.ShapeDtypeStruct(inputs[0].shape, BF16),
            jax.ShapeDtypeStruct(token.shape, token.dtype),
        ),
        in_specs=[VMEM] * len(inputs) + [ANY],
        out_specs=(VMEM, ANY),
        input_output_aliases={len(inputs): 1},
        compiler_params=params(),
        cost_estimate=cost(work * inputs[0].size, 3 * inputs[0].size),
        name="hop",
    )(*inputs, token)


def fold(rank, adapters, half):
    shape = (adapters * rank, 2 * rank)
    return (iota(shape, 0) % rank + half * rank == iota(shape, 1)).astype(BF16)


def slot_mask(tag, rank, adapters):
    shape = (tag.shape[0], adapters * rank)
    return (iota(shape, 1) // rank).astype(F32) == tag.astype(F32)


def low_kernel(rank, blocks, down, *refs):
    parts, low = refs[:blocks], refs[blocks + 1]
    adapters = down.shape[0] // rank
    feat = down.shape[1]
    rows = parts[0].shape[0]
    half = blocks // 2
    maps = down[...]
    folds = [fold(rank, adapters, h) for h in range(2)]
    for k in range(half):
        total = None
        for h in range(2):
            part = parts[h * half + k]
            wide = dot_cols(part[:, :feat], maps)
            kept = jnp.where(slot_mask(part[:, feat : feat + 1], rank, adapters), wide, 0.0)
            got = dot(kept.astype(BF16), folds[h])
            total = got if total is None else total + got
        low[k * rows : (k + 1) * rows, :] = total.astype(BF16)


def low_values(parts, down, rank, token):
    rows, width = parts[0].shape
    blocks = len(parts)
    return pl.pallas_call(
        functools.partial(low_kernel, rank, blocks),
        out_shape=(
            jax.ShapeDtypeStruct((blocks // 2 * rows, 2 * rank), BF16),
            jax.ShapeDtypeStruct(token.shape, token.dtype),
        ),
        in_specs=[VMEM] * (blocks + 1) + [ANY],
        out_specs=(VMEM, ANY),
        input_output_aliases={blocks + 1: 1},
        compiler_params=params(),
        name="low",
    )(down, *parts, token)


def delta_kernel(rank, blocks, sums, up, *refs):
    tags, lows, outs = refs[:blocks], refs[blocks : blocks + sums], refs[blocks + sums + 1 :]
    adapters = up.shape[0] // rank
    rows = tags[0].shape[0]
    half = blocks // 2
    total = lows[0][...].astype(F32)
    for other in lows[1:]:
        total = total + other[...].astype(F32)
    low = total.astype(BF16)
    maps = up[...]
    for h in range(2):
        spread = fold(rank, adapters, h)
        for k in range(half):
            wide = dot_cols(low[k * rows : (k + 1) * rows, :], spread)
            mask = slot_mask(tags[h * half + k][:, :1], rank, adapters)
            kept = jnp.where(mask, wide, 0.0).astype(BF16)
            outs[h * half + k][...] = dot(kept, maps).astype(BF16)


def delta_values(parts, lows, up, rank, token):
    rows, width = parts[0].shape
    blocks = len(parts)
    columns = up.shape[1]
    tag = pl.BlockSpec((rows, TAG), lambda i: (0, width // TAG - 1))
    whole = lambda a: pl.BlockSpec(a.shape, lambda i: (0, 0))
    return pl.pallas_call(
        functools.partial(delta_kernel, rank, blocks, len(lows)),
        out_shape=[jax.ShapeDtypeStruct((rows, columns), BF16)] * blocks
        + [jax.ShapeDtypeStruct(token.shape, token.dtype)],
        grid=(1,),
        in_specs=[whole(up)] + [tag] * blocks + [whole(a) for a in lows] + [ANY],
        out_specs=[pl.BlockSpec((rows, columns), lambda i: (0, 0))] * blocks + [ANY],
        input_output_aliases={1 + blocks + len(lows): blocks},
        compiler_params=params(),
        name="delta",
    )(up, *parts, *lows, token)


def add_delta_kernel(per, place, *refs):
    bases, refs = refs[: 2 * per], refs[2 * per :]
    outs, parts = refs[-2 * per - 1 : -1], refs[: -2 * per - 2]
    rows = parts[0].shape[0]
    inner = is_inner()
    widths = tuple(base.shape[1] for base in bases[:per])
    for j in range(per):
        column = column_at(j, widths)
        total = None
        for k, part in enumerate(parts):
            got = dot(place[:, k * rows : (k + 1) * rows], part[:, pl.ds(column, widths[j])])
            total = got if total is None else total + got
        for i, mine in ((j, inner), (per + j, jnp.logical_not(inner))):
            wide = bases[i][...].astype(F32)
            outs[i][...] = (wide + jnp.where(mine, total, 0.0)).astype(BF16)


def add_delta(bases, place, parts, token):
    per = len(bases) // 2
    inputs = [place, *bases, *parts]
    return pl.pallas_call(
        functools.partial(add_delta_kernel, per),
        out_shape=[jax.ShapeDtypeStruct(base.shape, BF16) for base in bases]
        + [jax.ShapeDtypeStruct(token.shape, token.dtype)],
        in_specs=[VMEM] * len(inputs) + [ANY],
        out_specs=[VMEM] * len(bases) + [ANY],
        input_output_aliases={len(inputs): len(bases)},
        compiler_params=params(),
        name="add_delta",
    )(*inputs, token)


def finish_kernel(widths, near_q, far_q, *refs):
    refs = list(refs)
    near = refs.pop(0) if near_q is not None else None
    far = refs.pop(0) if far_q is not None else None
    even, odd = refs.pop(0), refs.pop(0) if near_q is not None else None
    pick = refs.pop(0)
    out, _, made, sems = refs[-4:]

    def write(q, terms):
        column, width = column_at(q, widths), widths[q]
        cut = width // LANES // 2 * LANES
        copies = []
        for i, here in enumerate((slice(0, cut), slice(cut, width))):
            total = sum(term[:, here].astype(F32) for term in terms)
            made[:, here] = dot(pick[...], total.astype(BF16)).astype(BF16)
            there = pl.ds(pl.multiple_of(column + here.start, LANES), here.stop - here.start)
            copies.append(pltpu.make_async_copy(made.at[:, here], out.at[:, there], sems.at[i]))
            copies[-1].start()
        for copy in copies:
            copy.wait()

    if near_q is not None:

        @pl.when(is_inner())
        def _():
            write(near_q, [near, even, odd])

    if far_q is not None:

        @pl.when(jnp.logical_not(is_inner()))
        def _():
            write(far_q, [far, even])


def finish(near_q, far_q, widths, bases, even, odd, pick, held, token):
    rows, width = pick.shape[0], even.shape[1]
    inputs = [bases[q] for q in (near_q, far_q) if q is not None] + [even]
    inputs += [odd] if near_q is not None else []
    inputs += [pick]
    last = [token] if held is None else [held, token]
    aliases = {len(inputs) + len(last) - 1: 1}
    if held is not None:
        aliases[len(inputs)] = 0
    return pl.pallas_call(
        functools.partial(finish_kernel, widths, near_q, far_q),
        out_shape=(
            jax.ShapeDtypeStruct((rows, sum(widths)), BF16),
            jax.ShapeDtypeStruct(token.shape, token.dtype),
        ),
        in_specs=[VMEM] * len(inputs) + [ANY] * len(last),
        out_specs=(ANY, ANY),
        scratch_shapes=[pltpu.VMEM((rows, width), BF16), pltpu.SemaphoreType.DMA((2,))],
        input_output_aliases=aliases,
        compiler_params=params(),
        cost_estimate=cost(2 * LIVE_ROWS * rows * width, 6 * LIVE_ROWS * width),
        name="finish",
    )(*inputs, *last)


def send_groups(blocks):
    replicas = lax.axis_size("replica")
    parts = [blocks[0]]
    for k in range(1, replicas):
        hops = [(i, (i + k) % replicas) for i in range(replicas)]
        parts.append(lax.ppermute(blocks[k], "replica", hops))
    return parts


def send_lows(low):
    shards = lax.axis_size("tensor")
    if shards > 4:
        return [lax.psum(low, "tensor")]
    lows = [low]
    for k in range(1, shards):
        hops = [(i, (i + k) % shards) for i in range(shards)]
        lows.append(lax.ppermute(low, "tensor", hops))
    return lows


def send_back(made):
    replicas = lax.axis_size("replica")
    back = [made[0]]
    for k in range(1, replicas):
        hops = [(i, (i - k) % replicas) for i in range(replicas)]
        back.append(lax.ppermute(made[k], "replica", hops))
    return back


def on_device(x, owner, slot, live, weight, down, up):
    width = weight.shape[1]
    rank = down.shape[1]
    replicas, shards = lax.axis_size("replica"), lax.axis_size("tensor")
    down, up = down.reshape(-1, down.shape[2]), up.reshape(-1, up.shape[2])
    token = jnp.zeros((8, 128), jnp.int32)
    if shards != 4:
        compact_x, pick, place, *blocks = prepare(owner[:, 0], slot, live[0], x, replicas)
        z, share = lax.axis_index("tensor").astype(jnp.int32), width // shards
        base = dot(compact_x, weight)
        parts = send_groups(blocks)
        low, token = low_values(parts, down, rank, token)
        *made, token = delta_values(parts, send_lows(low), up, rank, token)
        back = jnp.concatenate(send_back(made), axis=0)
        mine = lax.dynamic_slice_in_dim(base, z * share, share, 1) + dot(place, back)
        base = lax.dynamic_update_slice_in_dim(base, mine, z * share, 1).astype(BF16)
        total = lax.psum_scatter(base, "tensor", scatter_dimension=1, tiled=True)
        total = lax.all_gather(total, "tensor", axis=1, tiled=True)
        return dot(pick, total).astype(BF16)

    widths = widths_of(width, shards)
    chunks, per = len(widths), len(widths) // shards
    even = [(0, 1), (1, 0), (2, 3), (3, 2)]
    odd = [(1, 2), (2, 1)]
    opened = prepare(owner[:, 0], slot, live[0], x, replicas, weight, widths)
    compact_x, pick, place, *blocks, message = opened
    evens, odds = {0: lax.ppermute(message, "tensor", even)}, {}
    parts = send_groups(blocks)
    first = (1, 2, chunks - 1)
    *early, token = base_chunks(first, widths, compact_x, weight, token)
    bases = {0: message, **dict(zip(first, early))}
    for step in (1, 2):
        evens[step] = lax.ppermute(bases[step], "tensor", even)
    message, token = hop(odd_hop_kernel, [bases[chunks - 1], evens[0]], token, FIRST_HOP_WORK)
    odds[1] = lax.ppermute(message, "tensor", odd)
    rest = tuple(range(3, chunks - 1))
    *late, token = base_chunks(rest, widths, compact_x, weight, token)
    bases.update(zip(rest, late))
    low, token = low_values(parts, down, rank, token)
    lows = send_lows(low)
    steps = chunks + 3
    result = None
    unfinished = list(range(steps))
    seen_even, seen_odd = set(), set()

    def close(result, token):
        for a in list(unfinished):
            b = chunks - a
            if a not in seen_even or (1 <= b <= chunks and b not in seen_odd):
                continue
            unfinished.remove(a)
            near_q = chunks - 1 - a if a < chunks else None
            far_q = chunks + 2 - a if a >= 3 else None
            result, token = finish(near_q, far_q, widths, bases, evens[a], odds.get(b), pick, result, token)
        return result, token

    for step in range(1, steps):
        if step >= 3:
            far = bases[step] if step < chunks else bases[step - 3]
            inputs = [bases[step - 3], far, odds[step - 2]]
            message, token = hop(even_hop_kernel, inputs, token)
            evens[step] = lax.ppermute(message, "tensor", even)
            seen_odd.add(step - 2)
            result, token = close(result, token)
        if 2 <= step <= chunks:
            message, token = hop(odd_hop_kernel, [bases[chunks - step], evens[step - 1]], token)
            odds[step] = lax.ppermute(message, "tensor", odd)
        seen_even.add(step - 1)
        if step == DELTA_AT:
            *made, token = delta_values(parts, lows, up, rank, token)
            back = send_back(made)
        if step == per + 2:
            own = list(range(per, 2 * per)) + list(range(3 * per, 4 * per))
            *summed, token = add_delta([bases[q] for q in own], place, back, token)
            for q, value in zip(own, summed):
                bases[q] = value
        result, token = close(result, token)
    seen_even.add(steps - 1)
    result, token = close(result, token)
    return result


def solution(mesh):
    placed = (
        P(("parts", "replica"), "tensor"),
        P(("parts", "replica"), None),
        P(("parts", "replica")),
        P(("parts", "replica"), None),
        P("tensor", None),
        P("replica", None, "tensor"),
        P("replica", None, "tensor"),
    )
    return jax.shard_map(
        on_device,
        mesh=mesh,
        in_specs=placed,
        out_specs=P(("parts", "replica"), None),
        check_vma=False,
    )
```

```python
import functools

import jax
import jax.numpy as jnp
from jax import lax
from jax.experimental import pallas as pl
from jax.experimental.pallas import tpu as pltpu
from jax.sharding import PartitionSpec as P

GROUP_ROWS = 16
CAP = 4
LIVE_ROWS = 224
TAG = 128
LANES = 128
CUTS = 3
BF16 = jnp.bfloat16
F32 = jnp.float32
MIB = 1024 * 1024
HOP_WORK = 8000
FIRST_HOP_WORK = 8000
BASE_WORK = 50000
PREPARE_MIB = 60
SPLIT = 3
DELTA_AT = 3


def dot(a, b):
    return jnp.dot(a, b, preferred_element_type=F32)


def dot_cols(a, b):
    return lax.dot_general(a, b, (((1,), (1,)), ((), ())), preferred_element_type=F32)


def iota(shape, dim):
    return lax.broadcasted_iota(jnp.int32, shape, dim)


def params(mib=50):
    return pltpu.CompilerParams(vmem_limit_bytes=mib * MIB)


def cost(flops, elements):
    return pl.CostEstimate(flops=flops, bytes_accessed=2 * elements, transcendentals=0)


ANY = pl.BlockSpec(memory_space=pl.ANY)
VMEM = pl.BlockSpec(memory_space=pltpu.VMEM)


def is_inner():
    z = lax.axis_index("tensor")
    return (z == 1) | (z == 2)


def widths_of(width, shards):
    tiles = width // shards // LANES
    if CUTS == 3:
        side = tiles // 3
        cuts = (side, tiles - 2 * side, side)
    else:
        cuts = (tiles // CUTS,) * CUTS
    return tuple(cut * LANES for cut in cuts) * shards


def column_at(q, widths):
    left, right = sum(widths[:q]), sum(widths[: len(widths) - 1 - q])
    column = jnp.where(lax.axis_index("tensor") % 2 == 0, right, left)
    return pl.multiple_of(column, LANES)


def weight_copy(w, q, widths, into, sem):
    return pltpu.make_async_copy(w.at[:, pl.ds(column_at(q, widths), widths[q])], into, sem)


def prepare_kernel(replicas, widths, owner_in, slot_in, live_in, x_in, *refs):
    refs = list(refs)
    line = widths is not None
    w = refs.pop(0) if line else None
    compact_x, pick, place = refs[:3]
    blocks = refs[3 : 3 + replicas]
    message = refs[3 + replicas] if line else None
    owner, slot, live, x, sems = refs[-5:]
    wide, wide_sem = (refs[-7], refs[-6]) if line else (None, None)
    copies = [
        pltpu.make_async_copy(src, dst, sems.at[i])
        for i, (src, dst) in enumerate(((owner_in, owner), (slot_in, slot), (live_in, live), (x_in, x)))
    ]
    for copy in copies:
        copy.start()
    if line:
        weights = weight_copy(w, 0, widths, wide, wide_sem.at[0])
        weights.start()
    for copy in copies:
        copy.wait()
    me = lax.axis_index("replica")
    rows, feat = x.shape
    groups = rows // GROUP_ROWS
    out_rows = replicas * CAP * GROUP_ROWS
    lane = iota((1, rows), 1)
    lane_group, lane_slot = lane // GROUP_ROWS, lane % GROUP_ROWS
    row_group = iota((rows, TAG), 0) // GROUP_ROWS
    packed = jnp.full((1, rows), -1, jnp.int32)
    target = jnp.zeros((1, rows), jnp.int32)
    tags = jnp.zeros((rows, TAG), F32)
    owners = [owner[g] for g in range(groups)]
    offset = jnp.int32(0)
    used = [jnp.int32(0)] * replicas
    for g in range(groups):
        count = live[g]
        mine = lane_group == g
        packed = jnp.where(mine & (lane_slot < count), offset + lane_slot, packed)
        offset = offset + count
        position = jnp.int32(0)
        for o in range(replicas):
            hit = owners[g] == o
            position = jnp.where(hit, used[o], position)
            used[o] = used[o] + hit.astype(jnp.int32)
        hop = lax.rem(owners[g] - me + replicas, replicas)
        start = (hop * CAP + position) * GROUP_ROWS
        target = jnp.where(mine, start + lane_slot, target)
        tags = jnp.where(row_group == g, slot[g].astype(F32), tags)
    compact = (iota((LIVE_ROWS, rows), 0) == packed).astype(BF16)
    spread = (iota((out_rows, rows), 0) == target).astype(BF16)
    pick[...] = compact.astype(F32).T.astype(BF16)
    place[...] = dot_cols(compact, spread).astype(BF16)
    packed_x = dot(compact, x[...]).astype(BF16)
    compact_x[...] = packed_x
    sent = dot(spread, x[...]).astype(BF16)
    sent_tags = dot(spread, tags.astype(BF16)).astype(BF16)
    for k, block in enumerate(blocks):
        here = slice(k * block.shape[0], (k + 1) * block.shape[0])
        block[:, :feat] = sent[here]
        block[:, feat:] = sent_tags[here]
    if line:
        weights.wait()
        message[...] = dot(packed_x, wide[...]).astype(BF16)


def prepare(owner, slot, live, x, replicas, weight=None, widths=None):
    rows, feat = x.shape
    block = CAP * GROUP_ROWS
    line = weight is not None
    shape = lambda *dims: jax.ShapeDtypeStruct(dims, BF16)
    outs = [shape(LIVE_ROWS, feat), shape(rows, LIVE_ROWS), shape(LIVE_ROWS, replicas * block)]
    outs += [shape(block, feat + TAG)] * replicas
    scratch = [pltpu.SMEM(a.shape, jnp.int32) for a in (owner, slot, live)]
    scratch += [pltpu.VMEM(x.shape, BF16), pltpu.SemaphoreType.DMA((4,))]
    if line:
        outs.append(shape(LIVE_ROWS, widths[0]))
        scratch = [pltpu.VMEM((feat, widths[0]), BF16), pltpu.SemaphoreType.DMA((1,))] + scratch
    return pl.pallas_call(
        functools.partial(prepare_kernel, replicas, widths),
        out_shape=outs,
        in_specs=[ANY] * (5 if line else 4),
        out_specs=[VMEM] * len(outs),
        scratch_shapes=scratch,
        compiler_params=params(PREPARE_MIB),
        name="prepare",
    )(owner, slot, live, x, *([weight] if line else []))


def base_kernel(places, widths, x, w, token_in, *refs):
    outs, wide, sems = refs[: len(places)], refs[-2], refs[-1]
    slots = wide.shape[0]
    copies = [
        weight_copy(w, q, widths, wide.at[i % slots, :, : widths[q]], sems.at[i % slots]) for i, q in enumerate(places)
    ]
    for copy in copies[: slots - 1]:
        copy.start()
    for i, (q, copy) in enumerate(zip(places, copies)):
        if i + slots - 1 < len(copies):
            copies[i + slots - 1].start()
        copy.wait()
        outs[i][...] = dot(x[...], wide[i % slots, :, : widths[q]]).astype(BF16)


def base_chunks(places, widths, x, weight, token):
    feat, _ = weight.shape
    columns = sum(widths[q] for q in places)
    return pl.pallas_call(
        functools.partial(base_kernel, places, widths),
        out_shape=[jax.ShapeDtypeStruct((LIVE_ROWS, widths[q]), BF16) for q in places]
        + [jax.ShapeDtypeStruct(token.shape, token.dtype)],
        in_specs=[VMEM, ANY, ANY],
        out_specs=[VMEM] * len(places) + [ANY],
        input_output_aliases={2: len(places)},
        scratch_shapes=[pltpu.VMEM((3, feat, max(widths)), BF16), pltpu.SemaphoreType.DMA((3,))],
        compiler_params=params(),
        cost_estimate=cost(BASE_WORK * columns, columns),
        name="base",
    )(x, weight, token)


def odd_hop_kernel(base, got, token_in, out, token):
    out[...] = (base[...].astype(F32) + got[...].astype(F32)).astype(BF16)


def even_hop_kernel(near, far, got, token_in, out, token):
    @pl.when(is_inner())
    def _():
        out[...] = (near[...].astype(F32) + got[...].astype(F32)).astype(BF16)

    @pl.when(jnp.logical_not(is_inner()))
    def _():
        out[...] = far[...]


def hop(kernel, inputs, token, work=HOP_WORK):
    return pl.pallas_call(
        kernel,
        out_shape=(
            jax.ShapeDtypeStruct(inputs[0].shape, BF16),
            jax.ShapeDtypeStruct(token.shape, token.dtype),
        ),
        in_specs=[VMEM] * len(inputs) + [ANY],
        out_specs=(VMEM, ANY),
        input_output_aliases={len(inputs): 1},
        compiler_params=params(),
        cost_estimate=cost(work * inputs[0].size, 3 * inputs[0].size),
        name="hop",
    )(*inputs, token)


def fold(rank, adapters, half):
    shape = (adapters * rank, 2 * rank)
    return (iota(shape, 0) % rank + half * rank == iota(shape, 1)).astype(BF16)


def slot_mask(tag, rank, adapters):
    shape = (tag.shape[0], adapters * rank)
    return (iota(shape, 1) // rank).astype(F32) == tag.astype(F32)


def low_kernel(rank, blocks, down, *refs):
    parts, low = refs[:blocks], refs[blocks + 1]
    adapters = down.shape[0] // rank
    feat = down.shape[1]
    rows = parts[0].shape[0]
    half = blocks // 2
    tall = jnp.concatenate([part[:, :feat] for part in parts], axis=0)
    tags = jnp.concatenate([part[:, feat:] for part in parts], axis=0)
    wide = dot_cols(tall, down[...])
    kept = jnp.where(slot_mask(tags[:, :1], rank, adapters), wide, 0.0).astype(BF16)
    cut = half * rows
    total = dot(kept[:cut], fold(rank, adapters, 0)) + dot(kept[cut:], fold(rank, adapters, 1))
    low[...] = total.astype(BF16)


def low_values(parts, down, rank, token):
    rows, width = parts[0].shape
    blocks = len(parts)
    return pl.pallas_call(
        functools.partial(low_kernel, rank, blocks),
        out_shape=(
            jax.ShapeDtypeStruct((blocks // 2 * rows, 2 * rank), BF16),
            jax.ShapeDtypeStruct(token.shape, token.dtype),
        ),
        in_specs=[VMEM] * (blocks + 1) + [ANY],
        out_specs=(VMEM, ANY),
        input_output_aliases={blocks + 1: 1},
        compiler_params=params(),
        name="low",
    )(down, *parts, token)


def delta_kernel(rank, blocks, sums, pieces, up, *refs):
    tags, lows, outs = refs[:blocks], refs[blocks : blocks + sums], refs[blocks + sums + 1 :]
    adapters = up.shape[0] // rank
    rows = tags[0].shape[0]
    widths = sum(pieces, ())
    total = lows[0][...].astype(F32)
    for other in lows[1:]:
        total = total + other[...].astype(F32)
    low = total.astype(BF16)
    wide = jnp.concatenate([dot_cols(low, fold(rank, adapters, h)) for h in range(2)], axis=0)
    tag = jnp.concatenate([block[...] for block in tags], axis=0)
    kept = jnp.where(slot_mask(tag[:, :1], rank, adapters), wide, 0.0).astype(BF16)
    j = 0
    for i, piece in enumerate(pieces):
        at = 0
        for width in piece:
            made = dot(kept, up[:, pl.ds(column_at(j, widths), width)]).astype(BF16)
            for k in range(blocks):
                outs[i * blocks + k][:, at : at + width] = made[k * rows : (k + 1) * rows]
            j, at = j + 1, at + width


def delta_values(parts, lows, up, rank, pieces, token):
    rows, width = parts[0].shape
    blocks = len(parts)
    tag = pl.BlockSpec((rows, TAG), lambda i: (0, width // TAG - 1))
    whole = lambda a: pl.BlockSpec(a.shape, lambda i: (0, 0))
    sizes = [sum(piece) for piece in pieces for _ in range(blocks)]
    *made, token = pl.pallas_call(
        functools.partial(delta_kernel, rank, blocks, len(lows), pieces),
        out_shape=[jax.ShapeDtypeStruct((rows, size), BF16) for size in sizes]
        + [jax.ShapeDtypeStruct(token.shape, token.dtype)],
        grid=(1,),
        in_specs=[whole(up)] + [tag] * blocks + [whole(a) for a in lows] + [ANY],
        out_specs=[pl.BlockSpec((rows, size), lambda i: (0, 0)) for size in sizes] + [ANY],
        input_output_aliases={1 + blocks + len(lows): len(sizes)},
        compiler_params=params(),
        name="delta",
    )(up, *parts, *lows, token)
    return [made[i * blocks : (i + 1) * blocks] for i in range(len(pieces))], token


def add_delta_kernel(per, place, *refs):
    bases, refs = refs[: 2 * per], refs[2 * per :]
    outs, parts = refs[-2 * per - 1 : -1], refs[: -2 * per - 2]
    inner = is_inner()
    column = 0
    for j in range(per):
        width = bases[j].shape[1]
        total = dot(place[...], jnp.concatenate([part[:, column : column + width] for part in parts], axis=0))
        for i, mine in ((j, inner), (per + j, jnp.logical_not(inner))):
            wide = bases[i][...].astype(F32)
            outs[i][...] = (wide + jnp.where(mine, total, 0.0)).astype(BF16)
        column = column + width


def add_delta(bases, place, parts, token):
    per = len(bases) // 2
    inputs = [place, *bases, *parts]
    return pl.pallas_call(
        functools.partial(add_delta_kernel, per),
        out_shape=[jax.ShapeDtypeStruct(base.shape, BF16) for base in bases]
        + [jax.ShapeDtypeStruct(token.shape, token.dtype)],
        in_specs=[VMEM] * len(inputs) + [ANY],
        out_specs=[VMEM] * len(bases) + [ANY],
        input_output_aliases={len(inputs): len(bases)},
        compiler_params=params(),
        name="add_delta",
    )(*inputs, token)


def finish_kernel(widths, near_q, far_q, *refs):
    refs = list(refs)
    near = refs.pop(0) if near_q is not None else None
    far = refs.pop(0) if far_q is not None else None
    even, odd = refs.pop(0), refs.pop(0) if near_q is not None else None
    pick = refs.pop(0)
    out, _, made, sems = refs[-4:]

    def write(q, terms):
        column, width = column_at(q, widths), widths[q]
        cut = width // LANES // 2 * LANES
        copies = []
        for i, here in enumerate((slice(0, cut), slice(cut, width))):
            total = sum(term[:, here].astype(F32) for term in terms)
            made[:, here] = dot(pick[...], total.astype(BF16)).astype(BF16)
            there = pl.ds(pl.multiple_of(column + here.start, LANES), here.stop - here.start)
            copies.append(pltpu.make_async_copy(made.at[:, here], out.at[:, there], sems.at[i]))
            copies[-1].start()
        for copy in copies:
            copy.wait()

    if near_q is not None:

        @pl.when(is_inner())
        def _():
            write(near_q, [near, even, odd])

    if far_q is not None:

        @pl.when(jnp.logical_not(is_inner()))
        def _():
            write(far_q, [far, even])


def finish(near_q, far_q, widths, bases, even, odd, pick, held, token):
    rows, width = pick.shape[0], even.shape[1]
    inputs = [bases[q] for q in (near_q, far_q) if q is not None] + [even]
    inputs += [odd] if near_q is not None else []
    inputs += [pick]
    last = [token] if held is None else [held, token]
    aliases = {len(inputs) + len(last) - 1: 1}
    if held is not None:
        aliases[len(inputs)] = 0
    return pl.pallas_call(
        functools.partial(finish_kernel, widths, near_q, far_q),
        out_shape=(
            jax.ShapeDtypeStruct((rows, sum(widths)), BF16),
            jax.ShapeDtypeStruct(token.shape, token.dtype),
        ),
        in_specs=[VMEM] * len(inputs) + [ANY] * len(last),
        out_specs=(ANY, ANY),
        scratch_shapes=[pltpu.VMEM((rows, width), BF16), pltpu.SemaphoreType.DMA((2,))],
        input_output_aliases=aliases,
        compiler_params=params(),
        cost_estimate=cost(2 * LIVE_ROWS * rows * width, 6 * LIVE_ROWS * width),
        name="finish",
    )(*inputs, *last)


def send_groups(blocks):
    replicas = lax.axis_size("replica")
    parts = [blocks[0]]
    for k in range(1, replicas):
        hops = [(i, (i + k) % replicas) for i in range(replicas)]
        parts.append(lax.ppermute(blocks[k], "replica", hops))
    return parts


def send_lows(low):
    shards = lax.axis_size("tensor")
    if shards > 4:
        return [lax.psum(low, "tensor")]
    lows = [low]
    for k in range(1, shards):
        hops = [(i, (i + k) % shards) for i in range(shards)]
        lows.append(lax.ppermute(low, "tensor", hops))
    return lows


def send_back(made):
    replicas = lax.axis_size("replica")
    back = [made[0]]
    for k in range(1, replicas):
        hops = [(i, (i - k) % replicas) for i in range(replicas)]
        back.append(lax.ppermute(made[k], "replica", hops))
    return back


def on_device(x, owner, slot, live, weight, down, up):
    width = weight.shape[1]
    rank = down.shape[1]
    replicas, shards = lax.axis_size("replica"), lax.axis_size("tensor")
    down, up = down.reshape(-1, down.shape[2]), up.reshape(-1, up.shape[2])
    token = jnp.zeros((8, 128), jnp.int32)
    if shards != 4:
        compact_x, pick, place, *blocks = prepare(owner[:, 0], slot, live[0], x, replicas)
        z, share = lax.axis_index("tensor").astype(jnp.int32), width // shards
        base = dot(compact_x, weight)
        parts = send_groups(blocks)
        low, token = low_values(parts, down, rank, token)
        (made,), token = delta_values(parts, send_lows(low), up, rank, ((share,),), token)
        back = jnp.concatenate(send_back(made), axis=0)
        mine = lax.dynamic_slice_in_dim(base, z * share, share, 1) + dot(place, back)
        base = lax.dynamic_update_slice_in_dim(base, mine, z * share, 1).astype(BF16)
        total = lax.psum_scatter(base, "tensor", scatter_dimension=1, tiled=True)
        total = lax.all_gather(total, "tensor", axis=1, tiled=True)
        return dot(pick, total).astype(BF16)

    widths = widths_of(width, shards)
    chunks, per = len(widths), len(widths) // shards
    even = [(0, 1), (1, 0), (2, 3), (3, 2)]
    odd = [(1, 2), (2, 1)]
    opened = prepare(owner[:, 0], slot, live[0], x, replicas, weight, widths)
    compact_x, pick, place, *blocks, message = opened
    evens, odds = {0: lax.ppermute(message, "tensor", even)}, {}
    parts = send_groups(blocks)
    first = (1, 2, chunks - 1)
    *early, token = base_chunks(first, widths, compact_x, weight, token)
    bases = {0: message, **dict(zip(first, early))}
    for step in (1, 2):
        evens[step] = lax.ppermute(bases[step], "tensor", even)
    message, token = hop(odd_hop_kernel, [bases[chunks - 1], evens[0]], token, FIRST_HOP_WORK)
    odds[1] = lax.ppermute(message, "tensor", odd)
    second = tuple(q for q in range(chunks) if q not in bases and (q <= DELTA_AT or q >= chunks - DELTA_AT))
    *late, token = base_chunks(second, widths, compact_x, weight, token)
    bases.update(zip(second, late))
    rest = tuple(q for q in range(chunks) if q not in bases)
    pieces = (widths[:SPLIT], widths[SPLIT:per]) if SPLIT < per else (widths[:per],)
    low, token = low_values(parts, down, rank, token)
    lows = send_lows(low)
    steps = chunks + 3
    result = None
    unfinished = list(range(steps))
    seen_even, seen_odd = set(), set()

    def close(result, token):
        for a in list(unfinished):
            b = chunks - a
            if a not in seen_even or (1 <= b <= chunks and b not in seen_odd):
                continue
            unfinished.remove(a)
            near_q = chunks - 1 - a if a < chunks else None
            far_q = chunks + 2 - a if a >= 3 else None
            result, token = finish(near_q, far_q, widths, bases, evens[a], odds.get(b), pick, result, token)
        return result, token

    for step in range(1, steps):
        if step >= 3:
            far = bases[step] if step < chunks else bases[step - 3]
            inputs = [bases[step - 3], far, odds[step - 2]]
            message, token = hop(even_hop_kernel, inputs, token)
            evens[step] = lax.ppermute(message, "tensor", even)
            seen_odd.add(step - 2)
            result, token = close(result, token)
        if 2 <= step <= chunks:
            message, token = hop(odd_hop_kernel, [bases[chunks - step], evens[step - 1]], token)
            odds[step] = lax.ppermute(message, "tensor", odd)
        seen_even.add(step - 1)
        if step == DELTA_AT:
            *late, token = base_chunks(rest, widths, compact_x, weight, token)
            bases.update(zip(rest, late))
            made, token = delta_values(parts, lows, up, rank, pieces, token)
            back = [send_back(blocks) for blocks in made]
        if 0 <= step - (per + 2) < len(pieces):
            i = step - (per + 2)
            here = range(sum(map(len, pieces[:i])), sum(map(len, pieces[: i + 1])))
            own = [per + j for j in here] + [3 * per + j for j in here]
            *summed, token = add_delta([bases[q] for q in own], place, back[i], token)
            for q, value in zip(own, summed):
                bases[q] = value
        result, token = close(result, token)
    seen_even.add(steps - 1)
    result, token = close(result, token)
    return result


def solution(mesh):
    placed = (
        P(("parts", "replica"), "tensor"),
        P(("parts", "replica"), None),
        P(("parts", "replica")),
        P(("parts", "replica"), None),
        P("tensor", None),
        P("replica", None, "tensor"),
        P("replica", None, "tensor"),
    )
    return jax.shard_map(
        on_device,
        mesh=mesh,
        in_specs=placed,
        out_specs=P(("parts", "replica"), None),
        check_vma=False,
    )
```

```python
import functools

import jax
import jax.numpy as jnp
from jax import lax
from jax.experimental import pallas as pl
from jax.experimental.pallas import tpu as pltpu
from jax.sharding import PartitionSpec as P

GROUP_ROWS = 16
CAP = 4
LIVE_ROWS = 224
TAG = 128
LANES = 128
CUTS = 3
BF16 = jnp.bfloat16
F32 = jnp.float32
MIB = 1024 * 1024
HOP_WORK = 8000
FIRST_HOP_WORK = 8000
BASE_WORK = 50000
PREPARE_MIB = 60
DELTA_AT = 3


def dot(a, b):
    return jnp.dot(a, b, preferred_element_type=F32)


def dot_cols(a, b):
    return lax.dot_general(a, b, (((1,), (1,)), ((), ())), preferred_element_type=F32)


def iota(shape, dim):
    return lax.broadcasted_iota(jnp.int32, shape, dim)


def params(mib=50):
    return pltpu.CompilerParams(vmem_limit_bytes=mib * MIB)


def cost(flops, elements):
    return pl.CostEstimate(flops=flops, bytes_accessed=2 * elements, transcendentals=0)


ANY = pl.BlockSpec(memory_space=pl.ANY)
VMEM = pl.BlockSpec(memory_space=pltpu.VMEM)


def is_inner():
    z = lax.axis_index("tensor")
    return (z == 1) | (z == 2)


def widths_of(width, shards):
    tiles = width // shards // LANES
    if CUTS == 3:
        side = tiles // 3
        cuts = (side, tiles - 2 * side, side)
    else:
        cuts = (tiles // CUTS,) * CUTS
    return tuple(cut * LANES for cut in cuts) * shards


def column_at(q, widths):
    left, right = sum(widths[:q]), sum(widths[: len(widths) - 1 - q])
    column = jnp.where(lax.axis_index("tensor") % 2 == 0, right, left)
    return pl.multiple_of(column, LANES)


def weight_copy(w, q, widths, into, sem):
    return pltpu.make_async_copy(w.at[:, pl.ds(column_at(q, widths), widths[q])], into, sem)


def prepare_kernel(replicas, widths, owner_in, slot_in, live_in, x_in, *refs):
    refs = list(refs)
    line = widths is not None
    w = refs.pop(0) if line else None
    compact_x, pick, place = refs[:3]
    blocks = refs[3 : 3 + replicas]
    message = refs[3 + replicas] if line else None
    owner, slot, live, x, sems = refs[-5:]
    wide, wide_sem = (refs[-7], refs[-6]) if line else (None, None)
    copies = [
        pltpu.make_async_copy(src, dst, sems.at[i])
        for i, (src, dst) in enumerate(((owner_in, owner), (slot_in, slot), (live_in, live), (x_in, x)))
    ]
    for copy in copies:
        copy.start()
    if line:
        weights = weight_copy(w, 0, widths, wide, wide_sem.at[0])
        weights.start()
    for copy in copies:
        copy.wait()
    me = lax.axis_index("replica")
    rows, feat = x.shape
    groups = rows // GROUP_ROWS
    out_rows = replicas * CAP * GROUP_ROWS
    lane = iota((1, rows), 1)
    lane_group, lane_slot = lane // GROUP_ROWS, lane % GROUP_ROWS
    row_group = iota((rows, TAG), 0) // GROUP_ROWS
    packed = jnp.full((1, rows), -1, jnp.int32)
    target = jnp.zeros((1, rows), jnp.int32)
    tags = jnp.zeros((rows, TAG), F32)
    owners = [owner[g] for g in range(groups)]
    offset = jnp.int32(0)
    used = [jnp.int32(0)] * replicas
    for g in range(groups):
        count = live[g]
        mine = lane_group == g
        packed = jnp.where(mine & (lane_slot < count), offset + lane_slot, packed)
        offset = offset + count
        position = jnp.int32(0)
        for o in range(replicas):
            hit = owners[g] == o
            position = jnp.where(hit, used[o], position)
            used[o] = used[o] + hit.astype(jnp.int32)
        hop = lax.rem(owners[g] - me + replicas, replicas)
        start = (hop * CAP + position) * GROUP_ROWS
        target = jnp.where(mine, start + lane_slot, target)
        tags = jnp.where(row_group == g, slot[g].astype(F32), tags)
    compact = (iota((LIVE_ROWS, rows), 0) == packed).astype(BF16)
    spread = (iota((out_rows, rows), 0) == target).astype(BF16)
    pick[...] = compact.astype(F32).T.astype(BF16)
    place[...] = dot_cols(compact, spread).astype(BF16)
    packed_x = dot(compact, x[...]).astype(BF16)
    compact_x[...] = packed_x
    sent = dot(spread, x[...]).astype(BF16)
    sent_tags = dot(spread, tags.astype(BF16)).astype(BF16)
    for k, block in enumerate(blocks):
        here = slice(k * block.shape[0], (k + 1) * block.shape[0])
        block[:, :feat] = sent[here]
        block[:, feat:] = sent_tags[here]
    if line:
        weights.wait()
        message[...] = dot(packed_x, wide[...]).astype(BF16)


def prepare(owner, slot, live, x, replicas, weight=None, widths=None):
    rows, feat = x.shape
    block = CAP * GROUP_ROWS
    line = weight is not None
    shape = lambda *dims: jax.ShapeDtypeStruct(dims, BF16)
    outs = [shape(LIVE_ROWS, feat), shape(rows, LIVE_ROWS), shape(LIVE_ROWS, replicas * block)]
    outs += [shape(block, feat + TAG)] * replicas
    scratch = [pltpu.SMEM(a.shape, jnp.int32) for a in (owner, slot, live)]
    scratch += [pltpu.VMEM(x.shape, BF16), pltpu.SemaphoreType.DMA((4,))]
    if line:
        outs.append(shape(LIVE_ROWS, widths[0]))
        scratch = [pltpu.VMEM((feat, widths[0]), BF16), pltpu.SemaphoreType.DMA((1,))] + scratch
    return pl.pallas_call(
        functools.partial(prepare_kernel, replicas, widths),
        out_shape=outs,
        in_specs=[ANY] * (5 if line else 4),
        out_specs=[VMEM] * len(outs),
        scratch_shapes=scratch,
        compiler_params=params(PREPARE_MIB),
        name="prepare",
    )(owner, slot, live, x, *([weight] if line else []))


def base_kernel(places, widths, x, w, token_in, *refs):
    outs, wide, sems = refs[: len(places)], refs[-2], refs[-1]
    slots = wide.shape[0]
    copies = [
        weight_copy(w, q, widths, wide.at[i % slots, :, : widths[q]], sems.at[i % slots]) for i, q in enumerate(places)
    ]
    for copy in copies[: slots - 1]:
        copy.start()
    for i, (q, copy) in enumerate(zip(places, copies)):
        if i + slots - 1 < len(copies):
            copies[i + slots - 1].start()
        copy.wait()
        outs[i][...] = dot(x[...], wide[i % slots, :, : widths[q]]).astype(BF16)


def base_chunks(places, widths, x, weight, token):
    feat, _ = weight.shape
    columns = sum(widths[q] for q in places)
    return pl.pallas_call(
        functools.partial(base_kernel, places, widths),
        out_shape=[jax.ShapeDtypeStruct((LIVE_ROWS, widths[q]), BF16) for q in places]
        + [jax.ShapeDtypeStruct(token.shape, token.dtype)],
        in_specs=[VMEM, ANY, ANY],
        out_specs=[VMEM] * len(places) + [ANY],
        input_output_aliases={2: len(places)},
        scratch_shapes=[pltpu.VMEM((3, feat, max(widths)), BF16), pltpu.SemaphoreType.DMA((3,))],
        compiler_params=params(),
        cost_estimate=cost(BASE_WORK * columns, columns),
        name="base",
    )(x, weight, token)


def odd_hop_kernel(base, got, token_in, out, token):
    out[...] = (base[...].astype(F32) + got[...].astype(F32)).astype(BF16)


def even_hop_kernel(near, far, got, token_in, out, token):
    @pl.when(is_inner())
    def _():
        out[...] = (near[...].astype(F32) + got[...].astype(F32)).astype(BF16)

    @pl.when(jnp.logical_not(is_inner()))
    def _():
        out[...] = far[...]


def hop(kernel, inputs, token, work=HOP_WORK):
    return pl.pallas_call(
        kernel,
        out_shape=(
            jax.ShapeDtypeStruct(inputs[0].shape, BF16),
            jax.ShapeDtypeStruct(token.shape, token.dtype),
        ),
        in_specs=[VMEM] * len(inputs) + [ANY],
        out_specs=(VMEM, ANY),
        input_output_aliases={len(inputs): 1},
        compiler_params=params(),
        cost_estimate=cost(work * inputs[0].size, 3 * inputs[0].size),
        name="hop",
    )(*inputs, token)


def fold(rank, adapters, half):
    shape = (adapters * rank, 2 * rank)
    return (iota(shape, 0) % rank + half * rank == iota(shape, 1)).astype(BF16)


def slot_mask(tag, rank, adapters):
    shape = (tag.shape[0], adapters * rank)
    return (iota(shape, 1) // rank).astype(F32) == tag.astype(F32)


def low_kernel(rank, blocks, down, *refs):
    parts, low = refs[:blocks], refs[blocks + 1]
    adapters = down.shape[0] // rank
    feat = down.shape[1]
    rows = parts[0].shape[0]
    half = blocks // 2
    tall = jnp.concatenate([part[:, :feat] for part in parts], axis=0)
    tags = jnp.concatenate([part[:, feat:] for part in parts], axis=0)
    wide = dot_cols(tall, down[...])
    kept = jnp.where(slot_mask(tags[:, :1], rank, adapters), wide, 0.0).astype(BF16)
    cut = half * rows
    total = dot(kept[:cut], fold(rank, adapters, 0)) + dot(kept[cut:], fold(rank, adapters, 1))
    low[...] = total.astype(BF16)


def low_values(parts, down, rank, token):
    rows, width = parts[0].shape
    blocks = len(parts)
    return pl.pallas_call(
        functools.partial(low_kernel, rank, blocks),
        out_shape=(
            jax.ShapeDtypeStruct((blocks // 2 * rows, 2 * rank), BF16),
            jax.ShapeDtypeStruct(token.shape, token.dtype),
        ),
        in_specs=[VMEM] * (blocks + 1) + [ANY],
        out_specs=(VMEM, ANY),
        input_output_aliases={blocks + 1: 1},
        compiler_params=params(),
        name="low",
    )(down, *parts, token)


def delta_kernel(rank, blocks, sums, pieces, up, *refs):
    tags, lows, outs = refs[:blocks], refs[blocks : blocks + sums], refs[blocks + sums + 1 :]
    adapters = up.shape[0] // rank
    rows = tags[0].shape[0]
    widths = sum(pieces, ())
    total = lows[0][...].astype(F32)
    for other in lows[1:]:
        total = total + other[...].astype(F32)
    low = total.astype(BF16)
    wide = jnp.concatenate([dot_cols(low, fold(rank, adapters, h)) for h in range(2)], axis=0)
    tag = jnp.concatenate([block[...] for block in tags], axis=0)
    kept = jnp.where(slot_mask(tag[:, :1], rank, adapters), wide, 0.0).astype(BF16)
    j = 0
    for i, piece in enumerate(pieces):
        at = 0
        for width in piece:
            made = dot(kept, up[:, pl.ds(column_at(j, widths), width)]).astype(BF16)
            for k in range(blocks):
                outs[i * blocks + k][:, at : at + width] = made[k * rows : (k + 1) * rows]
            j, at = j + 1, at + width


def delta_values(parts, lows, up, rank, pieces, token):
    rows, width = parts[0].shape
    blocks = len(parts)
    tag = pl.BlockSpec((rows, TAG), lambda i: (0, width // TAG - 1))
    whole = lambda a: pl.BlockSpec(a.shape, lambda i: (0, 0))
    sizes = [sum(piece) for piece in pieces for _ in range(blocks)]
    *made, token = pl.pallas_call(
        functools.partial(delta_kernel, rank, blocks, len(lows), pieces),
        out_shape=[jax.ShapeDtypeStruct((rows, size), BF16) for size in sizes]
        + [jax.ShapeDtypeStruct(token.shape, token.dtype)],
        grid=(1,),
        in_specs=[whole(up)] + [tag] * blocks + [whole(a) for a in lows] + [ANY],
        out_specs=[pl.BlockSpec((rows, size), lambda i: (0, 0)) for size in sizes] + [ANY],
        input_output_aliases={1 + blocks + len(lows): len(sizes)},
        compiler_params=params(),
        name="delta",
    )(up, *parts, *lows, token)
    return [made[i * blocks : (i + 1) * blocks] for i in range(len(pieces))], token


def add_delta_kernel(start, place, *refs):
    count = len(start) * 2
    bases, parts, outs = refs[:count], refs[count : -count - 2], refs[-count - 1 : -1]

    def add(i, j):
        base, out = bases[i], outs[i]
        here = slice(start[j], start[j] + base.shape[1])
        delta = dot(place[...], jnp.concatenate([part[:, here] for part in parts], axis=0))
        out[...] = (base[...].astype(F32) + delta).astype(BF16)

    @pl.when(is_inner())
    def _():
        for j in range(len(start)):
            add(j, j)

    @pl.when(jnp.logical_not(is_inner()))
    def _():
        for j in range(len(start)):
            add(len(start) + j, j)


def add_delta(bases, start, place, parts, token):
    inputs = [place, *bases, *parts]
    aliases = {1 + i: i for i in range(len(bases))}
    return pl.pallas_call(
        functools.partial(add_delta_kernel, start),
        out_shape=[jax.ShapeDtypeStruct(base.shape, BF16) for base in bases]
        + [jax.ShapeDtypeStruct(token.shape, token.dtype)],
        in_specs=[VMEM] * len(inputs) + [ANY],
        out_specs=[VMEM] * len(bases) + [ANY],
        input_output_aliases=aliases | {len(inputs): len(bases)},
        compiler_params=params(),
        name="add_delta",
    )(*inputs, token)


def finish_kernel(widths, near_q, far_q, *refs):
    refs = list(refs)
    near = refs.pop(0) if near_q is not None else None
    far = refs.pop(0) if far_q is not None else None
    even, odd = refs.pop(0), refs.pop(0) if near_q is not None else None
    pick = refs.pop(0)
    out, _, made, sems = refs[-4:]

    def write(q, terms):
        column, width = column_at(q, widths), widths[q]
        cut = width // LANES // 2 * LANES
        copies = []
        for i, here in enumerate((slice(0, cut), slice(cut, width))):
            total = sum(term[:, here].astype(F32) for term in terms)
            made[:, here] = dot(pick[...], total.astype(BF16)).astype(BF16)
            there = pl.ds(pl.multiple_of(column + here.start, LANES), here.stop - here.start)
            copies.append(pltpu.make_async_copy(made.at[:, here], out.at[:, there], sems.at[i]))
            copies[-1].start()
        for copy in copies:
            copy.wait()

    if near_q is not None:

        @pl.when(is_inner())
        def _():
            write(near_q, [near, even, odd])

    if far_q is not None:

        @pl.when(jnp.logical_not(is_inner()))
        def _():
            write(far_q, [far, even])


def finish(near_q, far_q, widths, bases, even, odd, pick, held, token):
    rows, width = pick.shape[0], even.shape[1]
    inputs = [bases[q] for q in (near_q, far_q) if q is not None] + [even]
    inputs += [odd] if near_q is not None else []
    inputs += [pick]
    last = [token] if held is None else [held, token]
    aliases = {len(inputs) + len(last) - 1: 1}
    if held is not None:
        aliases[len(inputs)] = 0
    return pl.pallas_call(
        functools.partial(finish_kernel, widths, near_q, far_q),
        out_shape=(
            jax.ShapeDtypeStruct((rows, sum(widths)), BF16),
            jax.ShapeDtypeStruct(token.shape, token.dtype),
        ),
        in_specs=[VMEM] * len(inputs) + [ANY] * len(last),
        out_specs=(ANY, ANY),
        scratch_shapes=[pltpu.VMEM((rows, width), BF16), pltpu.SemaphoreType.DMA((2,))],
        input_output_aliases=aliases,
        compiler_params=params(),
        cost_estimate=cost(2 * LIVE_ROWS * rows * width, 6 * LIVE_ROWS * width),
        name="finish",
    )(*inputs, *last)


def send_groups(blocks):
    replicas = lax.axis_size("replica")
    parts = [blocks[0]]
    for k in range(1, replicas):
        hops = [(i, (i + k) % replicas) for i in range(replicas)]
        parts.append(lax.ppermute(blocks[k], "replica", hops))
    return parts


def send_lows(low):
    shards = lax.axis_size("tensor")
    if shards > 4:
        return [lax.psum(low, "tensor")]
    lows = [low]
    for k in range(1, shards):
        hops = [(i, (i + k) % shards) for i in range(shards)]
        lows.append(lax.ppermute(low, "tensor", hops))
    return lows


def send_back(made):
    replicas = lax.axis_size("replica")
    back = [made[0]]
    for k in range(1, replicas):
        hops = [(i, (i - k) % replicas) for i in range(replicas)]
        back.append(lax.ppermute(made[k], "replica", hops))
    return back


def on_device(x, owner, slot, live, weight, down, up):
    width = weight.shape[1]
    rank = down.shape[1]
    replicas, shards = lax.axis_size("replica"), lax.axis_size("tensor")
    down, up = down.reshape(-1, down.shape[2]), up.reshape(-1, up.shape[2])
    token = jnp.zeros((8, 128), jnp.int32)
    if shards != 4:
        compact_x, pick, place, *blocks = prepare(owner[:, 0], slot, live[0], x, replicas)
        z, share = lax.axis_index("tensor").astype(jnp.int32), width // shards
        base = dot(compact_x, weight)
        parts = send_groups(blocks)
        low, token = low_values(parts, down, rank, token)
        (made,), token = delta_values(parts, send_lows(low), up, rank, ((share,),), token)
        back = jnp.concatenate(send_back(made), axis=0)
        mine = lax.dynamic_slice_in_dim(base, z * share, share, 1) + dot(place, back)
        base = lax.dynamic_update_slice_in_dim(base, mine, z * share, 1).astype(BF16)
        total = lax.psum_scatter(base, "tensor", scatter_dimension=1, tiled=True)
        total = lax.all_gather(total, "tensor", axis=1, tiled=True)
        return dot(pick, total).astype(BF16)

    widths = widths_of(width, shards)
    chunks, per = len(widths), len(widths) // shards
    even = [(0, 1), (1, 0), (2, 3), (3, 2)]
    odd = [(1, 2), (2, 1)]
    opened = prepare(owner[:, 0], slot, live[0], x, replicas, weight, widths)
    compact_x, pick, place, *blocks, message = opened
    evens, odds = {0: lax.ppermute(message, "tensor", even)}, {}
    parts = send_groups(blocks)
    first = (1, 2, chunks - 1)
    *early, token = base_chunks(first, widths, compact_x, weight, token)
    bases = {0: message, **dict(zip(first, early))}
    for step in (1, 2):
        evens[step] = lax.ppermute(bases[step], "tensor", even)
    message, token = hop(odd_hop_kernel, [bases[chunks - 1], evens[0]], token, FIRST_HOP_WORK)
    odds[1] = lax.ppermute(message, "tensor", odd)
    second = tuple(q for q in range(chunks) if q not in bases and (q <= DELTA_AT or q >= chunks - DELTA_AT))
    if second:
        *late, token = base_chunks(second, widths, compact_x, weight, token)
        bases.update(zip(second, late))
    rest = tuple(q for q in range(chunks) if q not in bases)
    pieces = (widths[:per],)
    low, token = low_values(parts, down, rank, token)
    lows = send_lows(low)
    steps = chunks + 3
    result = None
    unfinished = list(range(steps))
    seen_even, seen_odd = set(), set()

    def close(result, token):
        for a in list(unfinished):
            b = chunks - a
            if a not in seen_even or (1 <= b <= chunks and b not in seen_odd):
                continue
            unfinished.remove(a)
            near_q = chunks - 1 - a if a < chunks else None
            far_q = chunks + 2 - a if a >= 3 else None
            result, token = finish(near_q, far_q, widths, bases, evens[a], odds.get(b), pick, result, token)
        return result, token

    for step in range(1, steps):
        if step >= 3:
            far = bases[step] if step < chunks else bases[step - 3]
            inputs = [bases[step - 3], far, odds[step - 2]]
            message, token = hop(even_hop_kernel, inputs, token)
            evens[step] = lax.ppermute(message, "tensor", even)
            seen_odd.add(step - 2)
            result, token = close(result, token)
        if 2 <= step <= chunks:
            message, token = hop(odd_hop_kernel, [bases[chunks - step], evens[step - 1]], token)
            odds[step] = lax.ppermute(message, "tensor", odd)
        seen_even.add(step - 1)
        if step == DELTA_AT:
            *late, token = base_chunks(rest, widths, compact_x, weight, token)
            bases.update(zip(rest, late))
            made, token = delta_values(parts, lows, up, rank, pieces, token)
            back = [send_back(blocks) for blocks in made]
        if step == per + 2:
            own = list(range(per, 2 * per)) + list(range(3 * per, 4 * per))
            start = tuple(sum(widths[:j]) for j in range(per))
            *summed, token = add_delta([bases[q] for q in own], start, place, back[0], token)
            bases.update(zip(own, summed))
        result, token = close(result, token)
    seen_even.add(steps - 1)
    result, token = close(result, token)
    return result


def solution(mesh):
    placed = (
        P(("parts", "replica"), "tensor"),
        P(("parts", "replica"), None),
        P(("parts", "replica")),
        P(("parts", "replica"), None),
        P("tensor", None),
        P("replica", None, "tensor"),
        P("replica", None, "tensor"),
    )
    return jax.shard_map(
        on_device,
        mesh=mesh,
        in_specs=placed,
        out_specs=P(("parts", "replica"), None),
        check_vma=False,
    )
```
